32 devices in a mesh: groups: 2 (over x), wide: 8 (over z, y), narrow: 2 (over core).
Axes of the slice: x: 2, y: 2, z: 4, core: 2. Of those that a mesh axis runs over, the one named last changes fastest.
Arguments:
- tokens: bfloat16 [256, 8192], P(('groups', 'wide'), 'narrow'), parts along dimension 0, may hold values from -6 to 6
- gate_weight: bfloat16 [8192, 4096], P('narrow', 'wide'), may hold values from -0.0625 to 0.0625
- up_weight: bfloat16 [8192, 4096], P('narrow', 'wide'), may hold values from -0.0625 to 0.0625
- down_weight: bfloat16 [4096, 8192], P('wide', 'narrow'), may hold values from -0.09375 to 0.09375
Outputs:
- mixed: bfloat16 [256, 8192], P(('groups', 'wide'), 'narrow'), parts along dimension 0
The draws below stay inside these ranges and needn't reach their ends.
There are 2 independent parts, one for each index of `groups`. The reference program is written for one: setup_inputs(seed, part) draws one part's arguments, and reference() takes and returns one part's arrays. A program takes and returns all parts, laid end to end along the dimension named above; an argument that names none is the same for every part. Nothing has to cross between parts.
All inputs are finite; a program needn't handle non-finite values.
Results may differ from the reference program's by a relative error of at most 0.0049.
Values may be sent and summed in bfloat16 or wider, within the bound.
No kernel may reach another device: no remote copies, remote signals or barrier semaphores. Data moves between devices by JAX's collectives and lax.ppermute only.
A program may use at most 64 MiB of HBM per device.

```python
import jax
import jax.numpy as jnp

D_WIN = 8192
FF = 4096
TOKENS = 128


def steps_of(stream_key, shape, pieces, low, high):
    def one(axis_at, shards_of):
        heights = jax.random.uniform(jax.random.fold_in(jax.random.fold_in(stream_key, 6), axis_at), (shards_of,), jnp.float32, low / len(pieces), high / len(pieces))
        return jnp.repeat(jnp.exp(heights), shape[axis_at] // shards_of).reshape((-1,) + (1,) * (len(shape) - axis_at - 1))

    level = one(*pieces[0])
    for cut in pieces[1:]:
        level = level * one(*cut)
    return level


def scatter_about(rng, extent, spread, most, cuts=(), held_as=jnp.bfloat16):
    result = jax.random.normal(rng, extent, jnp.float32) * spread
    if len(cuts) > 0:
        result = steps_of(rng, extent, cuts, -0.22, 0.18) * result
    return jnp.clip(result, min=-most, max=most).astype(held_as)


def setup_inputs(seed: int = 0, part: int = 0) -> dict:
    arg_keys = jax.random.split(jax.random.key(seed), 5)
    own_keys = jax.random.split(jax.random.fold_in(arg_keys[4], part), 5)
    return {
        "tokens": scatter_about(own_keys[0], (TOKENS, D_WIN), 1.0, 6.0, ((0, 8), (1, 2))),
        "gate_weight": scatter_about(arg_keys[1], (D_WIN, FF), D_WIN ** -0.5, 0.0625, ((0, 2), (1, 8))),
        "up_weight": scatter_about(arg_keys[2], (D_WIN, FF), D_WIN ** -0.5, 0.0625, ((0, 2), (1, 8))),
        "down_weight": scatter_about(arg_keys[3], (FF, D_WIN), FF ** -0.5, 0.09375, ((0, 8), (1, 2))),
    }


def reference(tokens, gate_weight, up_weight, down_weight):
    gate_sum = jnp.dot(tokens, gate_weight, preferred_element_type=jnp.float32)
    up_sum = jnp.dot(tokens, up_weight, preferred_element_type=jnp.float32)
    hidden = (jax.nn.silu(gate_sum) * up_sum).astype(jnp.bfloat16)
    return jnp.dot(hidden, down_weight, preferred_element_type=jnp.float32).astype(jnp.bfloat16)
```

```python
import jax
import jax.numpy as jnp
from jax import lax
from jax.sharding import PartitionSpec as P

F32 = jnp.float32
BF16 = jnp.bfloat16


def make_local(wide, narrow):
    inner = 2 if wide % 2 == 0 else 1
    outer = wide // inner

    def along_outer(value, step):
        pairs = [(i, (i + step * inner) % wide) for i in range(wide)]
        return lax.ppermute(value, "wide", pairs)

    def along_inner(value):
        pairs = [(i, i ^ 1) for i in range(wide)]
        return lax.ppermute(value, "wide", pairs)

    def across_cores(value):
        pairs = [(i, (i + 1) % narrow) for i in range(narrow)]
        return lax.ppermute(value, "narrow", pairs)

    def local(tokens, gate_weight, up_weight, down_weight):
        rows = tokens.shape[0]
        mine = [tokens] + [along_outer(tokens, k) for k in range(1, outer)]
        theirs = [along_inner(block) for block in mine] if inner == 2 else []
        all_rows = jnp.concatenate(mine + theirs, axis=0)
        gate_part = jnp.dot(all_rows, gate_weight, preferred_element_type=F32)
        up_part = jnp.dot(all_rows, up_weight, preferred_element_type=F32)
        gate_sum = gate_part + across_cores(gate_part)
        up_sum = up_part + across_cores(up_part)
        hidden = (jax.nn.silu(gate_sum) * up_sum).astype(BF16)
        partial = jnp.dot(hidden, down_weight, preferred_element_type=F32)
        blocks = [partial[k * rows:(k + 1) * rows] for k in range(wide)]
        if inner == 2:
            paired = [
                blocks[k] + along_inner(blocks[outer + k].astype(BF16)).astype(F32)
                for k in range(outer)
            ]
        else:
            paired = blocks
        total = paired[0]
        for k in range(1, outer):
            total = total + along_outer(paired[k].astype(BF16), -k).astype(F32)
        return total.astype(BF16)

    return local


def solution(mesh):
    return jax.shard_map(
        make_local(mesh.shape["wide"], mesh.shape["narrow"]),
        mesh=mesh,
        in_specs=(
            P(("groups", "wide"), "narrow"),
            P("narrow", "wide"),
            P("narrow", "wide"),
            P("wide", "narrow"),
        ),
        out_specs=P(("groups", "wide"), "narrow"),
        check_vma=False,
    )
```

```python
import jax
import jax.numpy as jnp
from jax import lax
from jax.experimental import pallas as pl
from jax.experimental.pallas import tpu as pltpu
from jax.sharding import PartitionSpec as P

F32 = jnp.float32
BF16 = jnp.bfloat16


def pair_kernel(arrived_ref, own_ref, out_ref):
    out_ref[...] = (own_ref[...] + arrived_ref[...].astype(F32)).astype(out_ref.dtype)


def add_pair(arrived, own, dtype, flops):
    return pl.pallas_call(
        pair_kernel,
        out_shape=jax.ShapeDtypeStruct(own.shape, dtype),
        cost_estimate=pl.CostEstimate(flops=flops, bytes_accessed=0, transcendentals=0),
        name="add_pair",
    )(arrived, own)


def make_local(wide, narrow):
    inner = 2 if wide % 2 == 0 else 1
    outer = wide // inner

    def along_outer(value, step):
        pairs = [(i, (i + step * inner) % wide) for i in range(wide)]
        return lax.ppermute(value, "wide", pairs)

    def along_inner(value):
        pairs = [(i, i ^ 1) for i in range(wide)]
        return lax.ppermute(value, "wide", pairs)

    def across_cores(value):
        pairs = [(i, (i + 1) % narrow) for i in range(narrow)]
        return lax.ppermute(value, "narrow", pairs)

    def local(tokens, gate_weight, up_weight, down_weight):
        rows = tokens.shape[0]
        mine = [tokens] + [along_outer(tokens, k) for k in range(1, outer)]
        theirs = [along_inner(block) for block in mine] if inner == 2 else []
        all_rows = jnp.concatenate(mine + theirs, axis=0)
        gate_part = jnp.dot(all_rows, gate_weight, preferred_element_type=F32)
        up_part = jnp.dot(all_rows, up_weight, preferred_element_type=F32)
        gate_sum = gate_part + across_cores(gate_part)
        up_sum = up_part + across_cores(up_part)
        hidden = (jax.nn.silu(gate_sum) * up_sum).astype(BF16)
        partial = jnp.dot(hidden, down_weight, preferred_element_type=F32)
        blocks = [partial[k * rows:(k + 1) * rows] for k in range(wide)]
        order = sorted(range(1, outer), key=lambda k: -min(k, outer - k)) + [0]
        give = [blocks[outer + k].astype(BF16) for k in range(outer)] if inner == 2 else []
        sent = []
        for k in order:
            if inner == 2 and k == 0 and sent:
                give[0], sent[0] = lax.optimization_barrier((give[0], sent[0]))
            pair = blocks[k]
            if inner == 2:
                pair = add_pair(along_inner(give[k]), blocks[k], BF16 if k else F32, 1000000)
            if k:
                sent.append(pair.astype(BF16))
            else:
                total = pair
        for k, value in zip(order, sent):
            total = add_pair(along_outer(value, -k), total, BF16 if k == order[-2] else F32, 1500000000)
        return total

    return local


def solution(mesh):
    return jax.shard_map(
        make_local(mesh.shape["wide"], mesh.shape["narrow"]),
        mesh=mesh,
        in_specs=(
            P(("groups", "wide"), "narrow"),
            P("narrow", "wide"),
            P("narrow", "wide"),
            P("wide", "narrow"),
        ),
        out_specs=P(("groups", "wide"), "narrow"),
        check_vma=False,
    )
```

```python
import jax
import jax.numpy as jnp
from jax import lax
from jax.experimental import pallas as pl
from jax.experimental.pallas import tpu as pltpu
from jax.sharding import PartitionSpec as P

F32 = jnp.float32
BF16 = jnp.bfloat16


def pair_kernel(arrived_ref, own_ref, out_ref):
    out_ref[...] = (own_ref[...] + arrived_ref[...].astype(F32)).astype(out_ref.dtype)


def add_pair(arrived, own, dtype, flops):
    return pl.pallas_call(
        pair_kernel,
        out_shape=jax.ShapeDtypeStruct(own.shape, dtype),
        compiler_params=pltpu.CompilerParams(vmem_limit_bytes=2 << 20),
        cost_estimate=pl.CostEstimate(flops=flops, bytes_accessed=0, transcendentals=0),
        name="add_pair",
    )(arrived, own)


def make_local(wide, narrow):
    inner = 2 if wide % 2 == 0 else 1
    outer = wide // inner

    def along_outer(value, step):
        pairs = [(i, (i + step * inner) % wide) for i in range(wide)]
        return lax.ppermute(value, "wide", pairs)

    def along_inner(value):
        pairs = [(i, i ^ 1) for i in range(wide)]
        return lax.ppermute(value, "wide", pairs)

    def across_cores(value):
        pairs = [(i, (i + 1) % narrow) for i in range(narrow)]
        return lax.ppermute(value, "narrow", pairs)

    def local(tokens, gate_weight, up_weight, down_weight):
        rows = tokens.shape[0]
        mine = [tokens] + [along_outer(tokens, k) for k in range(1, outer)]
        theirs = [along_inner(block) for block in mine] if inner == 2 else []
        all_rows = jnp.concatenate(mine + theirs, axis=0)
        gate_part = jnp.dot(all_rows, gate_weight, preferred_element_type=F32)
        up_part = jnp.dot(all_rows, up_weight, preferred_element_type=F32)
        gate_sum = gate_part + across_cores(gate_part)
        up_sum = up_part + across_cores(up_part)
        hidden = (jax.nn.silu(gate_sum) * up_sum).astype(BF16)
        partial = jnp.dot(hidden, down_weight, preferred_element_type=F32)
        blocks = [partial[k * rows:(k + 1) * rows] for k in range(wide)]
        order = sorted(range(1, outer), key=lambda k: -min(k, outer - k)) + [0]
        give = [blocks[outer + k].astype(BF16) for k in range(outer)] if inner == 2 else []
        sent = []
        for k in order:
            if inner == 2 and k == 0 and sent:
                give[0], sent[0] = lax.optimization_barrier((give[0], sent[0]))
            pair = blocks[k]
            if inner == 2:
                pair = add_pair(along_inner(give[k]), blocks[k], BF16 if k else F32, 1000000)
            if k:
                sent.append(pair.astype(BF16))
            else:
                total = pair
        for k, value in zip(order, sent):
            total = add_pair(along_outer(value, -k), total, BF16 if k == order[-2] else F32, 1500000000)
        return total

    return local


def solution(mesh):
    return jax.shard_map(
        make_local(mesh.shape["wide"], mesh.shape["narrow"]),
        mesh=mesh,
        in_specs=(
            P(("groups", "wide"), "narrow"),
            P("narrow", "wide"),
            P("narrow", "wide"),
            P("wide", "narrow"),
        ),
        out_specs=P(("groups", "wide"), "narrow"),
        check_vma=False,
    )
```

```python
import functools

import jax
import jax.numpy as jnp
from jax import lax
from jax.experimental import pallas as pl
from jax.experimental.pallas import tpu as pltpu
from jax.sharding import PartitionSpec as P

F32 = jnp.float32
BF16 = jnp.bfloat16


def call(kernel, name, out_shape, flops, vmem, *operands):
    return pl.pallas_call(
        kernel,
        out_shape=out_shape,
        compiler_params=pltpu.CompilerParams(vmem_limit_bytes=vmem),
        cost_estimate=pl.CostEstimate(flops=flops, bytes_accessed=0, transcendentals=0),
        name=name,
    )(*operands)


def fetch_kernel(pieces, *refs):
    count = (len(refs) - 1) // 2
    sems = refs[-1]
    copies = []
    for n in range(count):
        source, target = refs[n], refs[count + n]
        step = source.shape[0] // pieces
        for i in range(pieces):
            part = pl.ds(i * step, step)
            copies.append(pltpu.make_async_copy(source.at[part], target.at[part], sems.at[n, i]))
    for copy in copies:
        copy.start()
    for copy in copies:
        copy.wait()


def fetch(weights, pieces=4):
    return pl.pallas_call(
        functools.partial(fetch_kernel, pieces),
        in_specs=[pl.BlockSpec(memory_space=pl.ANY)] * len(weights),
        out_specs=[pl.BlockSpec(memory_space=pltpu.VMEM)] * len(weights),
        out_shape=[jax.ShapeDtypeStruct(w.shape, w.dtype) for w in weights],
        scratch_shapes=[pltpu.SemaphoreType.DMA((len(weights), pieces))],
        compiler_params=pltpu.CompilerParams(vmem_limit_bytes=43 << 20),
        cost_estimate=pl.CostEstimate(flops=1000000000, bytes_accessed=0, transcendentals=0),
        name="fetch",
    )(*weights)


def project_kernel(*refs):
    *block_refs, weight_ref, out_ref = refs
    rows = jnp.concatenate([ref[...] for ref in block_refs], axis=0)
    out_ref[...] = jnp.dot(rows, weight_ref[...], preferred_element_type=F32)


def project(blocks, weight):
    rows = sum(block.shape[0] for block in blocks)
    out = jax.ShapeDtypeStruct((rows, weight.shape[1]), F32)
    flops = 2 * rows * weight.shape[0] * weight.shape[1]
    return call(project_kernel, "project", out, flops, 4 << 20, *blocks, weight)


def down_kernel(give, keep, gate_ref, gate_other_ref, up_ref, up_other_ref, weight_ref, *out_refs):
    gate_sum = gate_ref[...] + gate_other_ref[...]
    up_sum = up_ref[...] + up_other_ref[...]
    hidden = (jax.nn.silu(gate_sum) * up_sum).astype(BF16)
    width = weight_ref.shape[1]
    tile = min(512, width)
    rows = out_refs[0].shape[0]

    def column_tile(step, carry):
        columns = pl.ds(pl.multiple_of(step * tile, tile), tile)
        partial = jnp.dot(hidden, weight_ref[:, columns], preferred_element_type=F32)
        for k in range(keep + give):
            piece = partial[k * rows:(k + 1) * rows]
            out_refs[k][:, columns] = piece.astype(out_refs[k].dtype)
        return carry

    lax.fori_loop(0, width // tile, column_tile, 0, unroll=True)


def down(gate, gate_other, up, up_other, weight, rows, keep, give):
    width = weight.shape[1]
    outs = [jax.ShapeDtypeStruct((rows, width), F32)] * keep
    outs += [jax.ShapeDtypeStruct((rows, width), BF16)] * give
    flops = 2 * gate.shape[0] * weight.shape[0] * width
    return call(
        functools.partial(down_kernel, give, keep), "down", outs, flops, 4 << 20,
        gate, gate_other, up, up_other, weight,
    )


def pair_kernel(arrived_ref, own_ref, out_ref):
    out_ref[...] = (own_ref[...] + arrived_ref[...].astype(F32)).astype(out_ref.dtype)


def add_pair(arrived, own, dtype, flops):
    out = jax.ShapeDtypeStruct(own.shape, dtype)
    return call(pair_kernel, "add_pair", out, flops, 2 << 20, arrived, own)


def make_local(wide, narrow):
    inner = 2 if wide % 2 == 0 else 1
    outer = wide // inner

    def along_outer(value, step):
        pairs = [(i, (i + step * inner) % wide) for i in range(wide)]
        return lax.ppermute(value, "wide", pairs)

    def along_inner(value):
        pairs = [(i, i ^ 1) for i in range(wide)]
        return lax.ppermute(value, "wide", pairs)

    def across_cores(value):
        pairs = [(i, (i + 1) % narrow) for i in range(narrow)]
        return lax.ppermute(value, "narrow", pairs)

    def local(tokens, gate_weight, up_weight, down_weight):
        rows = tokens.shape[0]
        mine = [tokens] + [along_outer(tokens, k) for k in range(1, outer)]
        theirs = [along_inner(block) for block in mine] if inner == 2 else []
        gate_held, up_held = fetch([gate_weight, up_weight])
        gate_part = project(mine + theirs, gate_held)
        up_part = project(mine + theirs, up_held)
        blocks = down(
            gate_part, across_cores(gate_part), up_part, across_cores(up_part),
            down_weight, rows, len(mine), len(theirs),
        )
        order = sorted(range(1, outer), key=lambda k: -min(k, outer - k)) + [0]
        keep, give = list(blocks[:outer]), list(blocks[outer:])
        sent = []
        for k in order:
            if give and k == 0 and sent:
                give[0], sent[0] = lax.optimization_barrier((give[0], sent[0]))
            pair = keep[k]
            if give:
                pair = add_pair(along_inner(give[k]), keep[k], BF16 if k else F32, 1000000)
            if k:
                sent.append(pair.astype(BF16))
            else:
                total = pair
        for k, value in zip(order, sent):
            last = k == order[-2]
            total = add_pair(along_outer(value, -k), total, BF16 if last else F32, 1500000000)
        return total.astype(BF16)

    return local


def solution(mesh):
    return jax.shard_map(
        make_local(mesh.shape["wide"], mesh.shape["narrow"]),
        mesh=mesh,
        in_specs=(
            P(("groups", "wide"), "narrow"),
            P("narrow", "wide"),
            P("narrow", "wide"),
            P("wide", "narrow"),
        ),
        out_specs=P(("groups", "wide"), "narrow"),
        check_vma=False,
    )
```

```python
import functools

import jax
import jax.numpy as jnp
from jax import lax
from jax.experimental import pallas as pl
from jax.experimental.pallas import tpu as pltpu
from jax.sharding import PartitionSpec as P

F32 = jnp.float32
BF16 = jnp.bfloat16


def call(kernel, name, out_shape, flops, vmem, *operands):
    return pl.pallas_call(
        kernel,
        out_shape=out_shape,
        compiler_params=pltpu.CompilerParams(vmem_limit_bytes=vmem),
        cost_estimate=pl.CostEstimate(flops=flops, bytes_accessed=0, transcendentals=0),
        name=name,
    )(*operands)


def fetch_kernel(pieces, *refs):
    count = (len(refs) - 1) // 2
    sems = refs[-1]
    copies = []
    for n in range(count):
        source, target = refs[n], refs[count + n]
        step = source.shape[0] // pieces
        for i in range(pieces):
            part = pl.ds(i * step, step)
            copies.append(pltpu.make_async_copy(source.at[part], target.at[part], sems.at[n, i]))
    for copy in copies:
        copy.start()
    for copy in copies:
        copy.wait()


def fetch(weights, pieces=4):
    return pl.pallas_call(
        functools.partial(fetch_kernel, pieces),
        in_specs=[pl.BlockSpec(memory_space=pl.ANY)] * len(weights),
        out_specs=[pl.BlockSpec(memory_space=pltpu.VMEM)] * len(weights),
        out_shape=[jax.ShapeDtypeStruct(w.shape, w.dtype) for w in weights],
        scratch_shapes=[pltpu.SemaphoreType.DMA((len(weights), pieces))],
        compiler_params=pltpu.CompilerParams(vmem_limit_bytes=43 << 20),
        cost_estimate=pl.CostEstimate(flops=1000000000, bytes_accessed=0, transcendentals=0),
        name="fetch",
    )(*weights)


def project_kernel(*refs):
    *block_refs, weight_ref, out_ref = refs
    rows = jnp.concatenate([ref[...] for ref in block_refs], axis=0)
    out_ref[...] = jnp.dot(rows, weight_ref[...], preferred_element_type=F32)


def project(blocks, weight):
    rows = sum(block.shape[0] for block in blocks)
    out = jax.ShapeDtypeStruct((rows, weight.shape[1]), F32)
    flops = 2 * rows * weight.shape[0] * weight.shape[1]
    return call(project_kernel, "project", out, flops, 4 << 20, *blocks, weight)


def down_kernel(give, keep, gate_ref, gate_other_ref, up_ref, up_other_ref, weight_ref, *out_refs):
    gate_sum = gate_ref[...] + gate_other_ref[...]
    up_sum = up_ref[...] + up_other_ref[...]
    hidden = (jax.nn.silu(gate_sum) * up_sum).astype(BF16)
    width = weight_ref.shape[1]
    tile = min(512, width)
    rows = out_refs[0].shape[0]

    def column_tile(step, carry):
        columns = pl.ds(pl.multiple_of(step * tile, tile), tile)
        partial = jnp.dot(hidden, weight_ref[:, columns], preferred_element_type=F32)
        for k in range(keep + give):
            piece = partial[k * rows:(k + 1) * rows]
            out_refs[k][:, columns] = piece.astype(out_refs[k].dtype)
        return carry

    lax.fori_loop(0, width // tile, column_tile, 0, unroll=True)


def down(gate, gate_other, up, up_other, weight, rows, keep, give):
    width = weight.shape[1]
    outs = [jax.ShapeDtypeStruct((rows, width), F32)] * keep
    outs += [jax.ShapeDtypeStruct((rows, width), BF16)] * give
    flops = 2 * gate.shape[0] * weight.shape[0] * width
    return call(
        functools.partial(down_kernel, give, keep), "down", outs, flops, 4 << 20,
        gate, gate_other, up, up_other, weight,
    )


def pair_kernel(arrived_ref, own_ref, out_ref):
    out_ref[...] = (own_ref[...] + arrived_ref[...].astype(F32)).astype(out_ref.dtype)


def add_pair(arrived, own, dtype, flops):
    out = jax.ShapeDtypeStruct(own.shape, dtype)
    return call(pair_kernel, "add_pair", out, flops, 2 << 20, arrived, own)


def make_local(wide, narrow):
    inner = 2 if wide % 2 == 0 else 1
    outer = wide // inner

    def along_outer(value, step):
        pairs = [(i, (i + step * inner) % wide) for i in range(wide)]
        return lax.ppermute(value, "wide", pairs)

    def along_inner(value):
        pairs = [(i, i ^ 1) for i in range(wide)]
        return lax.ppermute(value, "wide", pairs)

    def across_cores(value):
        pairs = [(i, (i + 1) % narrow) for i in range(narrow)]
        return lax.ppermute(value, "narrow", pairs)

    shifts = sorted(range(outer), key=lambda k: (min(k, outer - k), k))
    near = [k for k in shifts if min(k, outer - k) <= outer // 4]
    waves = [near, [k for k in shifts if k not in near]]

    def local(tokens, gate_weight, up_weight, down_weight):
        rows = tokens.shape[0]
        mine = {k: along_outer(tokens, k) if k else tokens for k in shifts}
        theirs = {k: along_inner(mine[k]) for k in shifts} if inner == 2 else {}
        gate_held, up_held = fetch([gate_weight, up_weight])
        keep, give = {}, {}
        for wave in waves:
            if not wave:
                continue
            blocks = [mine[k] for k in wave] + [theirs[k] for k in wave if theirs]
            gate_part = project(blocks, gate_held)
            up_part = project(blocks, up_held)
            outs = down(
                gate_part, across_cores(gate_part), up_part, across_cores(up_part),
                down_weight, rows, len(wave), len(blocks) - len(wave),
            )
            keep.update(zip(wave, outs[:len(wave)]))
            give.update(zip(wave, outs[len(wave):]))
        total = None
        for k in shifts:
            last = k == shifts[-1]
            pair = keep[k]
            if give:
                pair = add_pair(along_inner(give[k]), keep[k], BF16 if k else F32, 1000000)
            if k:
                arrived = along_outer(pair.astype(BF16), -k)
                hint = 100000000 if k == shifts[1] else 5000000000
                total = add_pair(arrived, total, BF16 if last else F32, hint)
            else:
                total = pair
        return total.astype(BF16)

    return local


def solution(mesh):
    return jax.shard_map(
        make_local(mesh.shape["wide"], mesh.shape["narrow"]),
        mesh=mesh,
        in_specs=(
            P(("groups", "wide"), "narrow"),
            P("narrow", "wide"),
            P("narrow", "wide"),
            P("wide", "narrow"),
        ),
        out_specs=P(("groups", "wide"), "narrow"),
        check_vma=False,
    )
```

```python
import functools

import jax
import jax.numpy as jnp
from jax import lax
from jax.experimental import pallas as pl
from jax.experimental.pallas import tpu as pltpu
from jax.sharding import PartitionSpec as P

F32 = jnp.float32
BF16 = jnp.bfloat16


def call(kernel, name, out_shape, flops, vmem, *operands):
    return pl.pallas_call(
        kernel,
        out_shape=out_shape,
        compiler_params=pltpu.CompilerParams(vmem_limit_bytes=vmem),
        cost_estimate=pl.CostEstimate(flops=flops, bytes_accessed=0, transcendentals=0),
        name=name,
    )(*operands)


def fetch_kernel(pieces, *refs):
    count = (len(refs) - 1) // 2
    sems = refs[-1]
    copies = []
    for n in range(count):
        source, target = refs[n], refs[count + n]
        step = source.shape[0] // pieces
        for i in range(pieces):
            part = pl.ds(i * step, step)
            copies.append(pltpu.make_async_copy(source.at[part], target.at[part], sems.at[n, i]))
    for copy in copies:
        copy.start()
    for copy in copies:
        copy.wait()


def fetch(weights, pieces=4):
    return pl.pallas_call(
        functools.partial(fetch_kernel, pieces),
        in_specs=[pl.BlockSpec(memory_space=pl.ANY)] * len(weights),
        out_specs=[pl.BlockSpec(memory_space=pltpu.VMEM)] * len(weights),
        out_shape=[jax.ShapeDtypeStruct(w.shape, w.dtype) for w in weights],
        scratch_shapes=[pltpu.SemaphoreType.DMA((len(weights), pieces))],
        compiler_params=pltpu.CompilerParams(vmem_limit_bytes=43 << 20),
        cost_estimate=pl.CostEstimate(flops=1000000000, bytes_accessed=0, transcendentals=0),
        name="fetch",
    )(*weights)


def project_kernel(*refs):
    *block_refs, weight_ref, out_ref = refs
    rows = jnp.concatenate([ref[...] for ref in block_refs], axis=0)
    out_ref[...] = jnp.dot(rows, weight_ref[...], preferred_element_type=F32)


def project(blocks, weight):
    rows = sum(block.shape[0] for block in blocks)
    out = jax.ShapeDtypeStruct((rows, weight.shape[1]), F32)
    return call(project_kernel, "project", out, 2000000000, 4 << 20, *blocks, weight)


def down_kernel(give, keep, gate_ref, gate_other_ref, up_ref, up_other_ref, weight_ref, *out_refs):
    gate_sum = gate_ref[...] + gate_other_ref[...]
    up_sum = up_ref[...] + up_other_ref[...]
    hidden = (jax.nn.silu(gate_sum) * up_sum).astype(BF16)
    width = weight_ref.shape[1]
    tile = min(512, width)
    rows = out_refs[0].shape[0]

    def column_tile(step, carry):
        columns = pl.ds(pl.multiple_of(step * tile, tile), tile)
        partial = jnp.dot(hidden, weight_ref[:, columns], preferred_element_type=F32)
        for k in range(keep + give):
            piece = partial[k * rows:(k + 1) * rows]
            out_refs[k][:, columns] = piece.astype(out_refs[k].dtype)
        return carry

    lax.fori_loop(0, width // tile, column_tile, 0, unroll=True)


def down(gate, gate_other, up, up_other, weight, rows, keep, give):
    width = weight.shape[1]
    outs = [jax.ShapeDtypeStruct((rows, width), F32)] * keep
    outs += [jax.ShapeDtypeStruct((rows, width), BF16)] * give
    flops = 2 * gate.shape[0] * weight.shape[0] * width
    return call(
        functools.partial(down_kernel, give, keep), "down", outs, flops, 4 << 20,
        gate, gate_other, up, up_other, weight,
    )


def pair_kernel(arrived_ref, own_ref, *refs):
    out_ref = refs[-1]
    out_ref[...] = (own_ref[...] + arrived_ref[...].astype(F32)).astype(out_ref.dtype)


def add_pair(arrived, own, dtype, flops, after=()):
    return pl.pallas_call(
        pair_kernel,
        in_specs=[pl.BlockSpec(memory_space=pltpu.VMEM)] * 2
        + [pl.BlockSpec(memory_space=pl.ANY)] * len(after),
        out_shape=jax.ShapeDtypeStruct(own.shape, dtype),
        compiler_params=pltpu.CompilerParams(vmem_limit_bytes=2 << 20),
        cost_estimate=pl.CostEstimate(flops=flops, bytes_accessed=0, transcendentals=0),
        name="add_pair",
    )(arrived, own, *after)


def make_local(wide, narrow):
    inner = 2
    outer = wide // inner

    pairwise = outer & (outer - 1) == 0

    def along_outer(value, k, back=False):
        if pairwise:
            pairs = [(i, i ^ (k * inner)) for i in range(wide)]
        else:
            pairs = [(i, (i + (-k if back else k) * inner) % wide) for i in range(wide)]
        return lax.ppermute(value, "wide", pairs)

    def along_inner(value):
        pairs = [(i, i ^ 1) for i in range(wide)]
        return lax.ppermute(value, "wide", pairs)

    def across_cores(value):
        pairs = [(i, (i + 1) % narrow) for i in range(narrow)]
        return lax.ppermute(value, "narrow", pairs)

    split = max(outer * 3 // 4, 1)
    waves = [[0] + list(range(split - 1, 0, -1)), list(range(split, outer))]

    def local(tokens, gate_weight, up_weight, down_weight):
        rows = tokens.shape[0]
        mine = {k: along_outer(tokens, k) if k else tokens for k in range(outer)}
        theirs = {k: along_inner(mine[k]) for k in range(outer)}
        gate_held, up_held = fetch([gate_weight, up_weight])
        keep, give = {}, {}
        for wave in waves:
            if not wave:
                continue
            blocks = [mine[k] for k in wave] + [theirs[k] for k in wave]
            gate_part = project(blocks, gate_held)
            up_part = project(blocks, up_held)
            outs = down(
                gate_part, across_cores(gate_part), up_part, across_cores(up_part),
                down_weight, rows, len(wave), len(wave),
            )
            keep.update(zip(wave, outs[:len(wave)]))
            give.update(zip(wave, outs[len(wave):]))
        def send_back(k, after=()):
            pair = add_pair(along_inner(give[k]), keep[k], BF16, 1000000, after)
            return along_outer(pair, k, back=True)

        near, far = waves[0][1:], waves[1]
        arrived = {k: send_back(k) for k in near}
        total = keep[0]
        after = ()
        for k in near:
            total = add_pair(arrived[k], total, F32, 3000000000)
            after = after or (total,)
        arrived.update({k: send_back(k, after) for k in far})
        total = add_pair(along_inner(give[0]), total, F32, 100000000)
        for k in far:
            total = add_pair(arrived[k], total, BF16 if k == far[-1] else F32, 5000000000)
        return total.astype(BF16)

    return local


def solution(mesh):
    return jax.shard_map(
        make_local(mesh.shape["wide"], mesh.shape["narrow"]),
        mesh=mesh,
        in_specs=(
            P(("groups", "wide"), "narrow"),
            P("narrow", "wide"),
            P("narrow", "wide"),
            P("wide", "narrow"),
        ),
        out_specs=P(("groups", "wide"), "narrow"),
        check_vma=False,
    )
```

```python
import functools

import jax
import jax.numpy as jnp
from jax import lax
from jax.experimental import pallas as pl
from jax.experimental.pallas import tpu as pltpu
from jax.sharding import PartitionSpec as P

F32 = jnp.float32
BF16 = jnp.bfloat16


def call(kernel, name, out_shape, flops, vmem, *operands):
    return pl.pallas_call(
        kernel,
        out_shape=out_shape,
        compiler_params=pltpu.CompilerParams(vmem_limit_bytes=vmem),
        cost_estimate=pl.CostEstimate(flops=flops, bytes_accessed=0, transcendentals=0),
        name=name,
    )(*operands)


def fetch_kernel(pieces, count, *refs):
    sources, targets, sems = refs[:count], refs[-1 - count:-1], refs[-1]
    copies = []
    for n, (source, target) in enumerate(zip(sources, targets)):
        step = source.shape[0] // pieces
        for i in range(pieces):
            part = pl.ds(i * step, step)
            copies.append(pltpu.make_async_copy(source.at[part], target.at[part], sems.at[n, i]))
    for copy in copies:
        copy.start()
    for copy in copies:
        copy.wait()


def fetch(weights, after, pieces=4):
    count = len(weights)
    return pl.pallas_call(
        functools.partial(fetch_kernel, pieces, count),
        in_specs=[pl.BlockSpec(memory_space=pl.ANY)] * (count + len(after)),
        out_specs=[pl.BlockSpec(memory_space=pltpu.VMEM)] * count,
        out_shape=[jax.ShapeDtypeStruct(w.shape, w.dtype) for w in weights],
        scratch_shapes=[pltpu.SemaphoreType.DMA((count, pieces))],
        compiler_params=pltpu.CompilerParams(vmem_limit_bytes=43 << 20),
        cost_estimate=pl.CostEstimate(flops=4000000000, bytes_accessed=0, transcendentals=0),
        name="fetch",
    )(*weights, *after)


def project_kernel(*refs):
    *block_refs, weight_ref, out_ref = refs
    rows = jnp.concatenate([ref[...] for ref in block_refs], axis=0)
    out_ref[...] = jnp.dot(rows, weight_ref[...], preferred_element_type=F32)


def project(blocks, weight):
    rows = sum(block.shape[0] for block in blocks)
    out = jax.ShapeDtypeStruct((rows, weight.shape[1]), F32)
    return call(project_kernel, "project", out, 400000000, 4 << 20, *blocks, weight)


def down_kernel(give, keep, gate_ref, gate_other_ref, up_ref, up_other_ref, weight_ref, *out_refs):
    gate_sum = gate_ref[...] + gate_other_ref[...]
    up_sum = up_ref[...] + up_other_ref[...]
    hidden = (jax.nn.silu(gate_sum) * up_sum).astype(BF16)
    width = weight_ref.shape[1]
    tile = min(512, width)
    rows = out_refs[0].shape[0]

    def column_tile(step, carry):
        columns = pl.ds(pl.multiple_of(step * tile, tile), tile)
        partial = jnp.dot(hidden, weight_ref[:, columns], preferred_element_type=F32)
        for k in range(keep + give):
            piece = partial[k * rows:(k + 1) * rows]
            out_refs[k][:, columns] = piece.astype(out_refs[k].dtype)
        return carry

    lax.fori_loop(0, width // tile, column_tile, 0, unroll=True)


def down(gate, gate_other, up, up_other, weight, rows, keep, give):
    width = weight.shape[1]
    outs = [jax.ShapeDtypeStruct((rows, width), F32)] * keep
    outs += [jax.ShapeDtypeStruct((rows, width), BF16)] * give
    flops = 2 * gate.shape[0] * weight.shape[0] * width
    return call(
        functools.partial(down_kernel, give, keep), "down", outs, flops, 4 << 20,
        gate, gate_other, up, up_other, weight,
    )


def add_kernel(count, own_ref, *refs):
    total = own_ref[...]
    for ref in refs[:count]:
        total = total + ref[...].astype(F32)
    refs[-1][...] = total.astype(refs[-1].dtype)


def add(own, arrived, dtype, hint=1000000, after=()):
    count = len(arrived)
    return pl.pallas_call(
        functools.partial(add_kernel, count),
        in_specs=[pl.BlockSpec(memory_space=pltpu.VMEM)] * (1 + count)
        + [pl.BlockSpec(memory_space=pl.ANY)] * len(after),
        out_shape=jax.ShapeDtypeStruct(own.shape, dtype),
        compiler_params=pltpu.CompilerParams(vmem_limit_bytes=2 << 20),
        cost_estimate=pl.CostEstimate(flops=hint, bytes_accessed=0, transcendentals=0),
        name="add",
    )(own, *arrived, *after)


def make_local(wide, narrow):
    fars = list(range(4, wide, 4))

    def swap(value, bits):
        return lax.ppermute(value, "wide", [(i, i ^ bits) for i in range(wide)])

    def across_cores(value):
        return lax.ppermute(value, "narrow", [(i, (i + 1) % narrow) for i in range(narrow)])

    def local(tokens, gate_weight, up_weight, down_weight):
        rows = tokens.shape[0]
        block = {0: tokens}
        for far in fars:
            block[far] = swap(tokens, far)
        block[2] = swap(tokens, 2)
        block[1] = swap(tokens, 1)
        block[2], block[1] = lax.optimization_barrier((block[2], block[1]))
        block[3] = swap(block[2], 1)
        for far in fars:
            for near in (2, 3, 1):
                block[far + near] = swap(block[far], near)
        gate_held, up_held = fetch([gate_weight, up_weight], [block[3]])
        stay = [0, 2] + fars
        away = [b for b in range(wide) if b not in stay]
        blocks = [block[b] for b in stay + away]
        gate_part = project(blocks, gate_held)
        up_part = project(blocks, up_held)
        outs = down(
            gate_part, across_cores(gate_part), up_part, across_cores(up_part),
            down_weight, rows, len(stay), len(away),
        )
        part = dict(zip(stay + away, outs))
        sums = []
        for far in fars:
            quad = [swap(part[far + near], near) for near in (2, 3, 1)]
            sums.append(add(part[far], quad, BF16))
        arrived = [swap(value, far) for value, far in zip(sums, fars)]
        pair = add(part[2], [swap(part[3], 1)], BF16, after=sums)
        total = add(part[0], arrived, F32, 1500000000)
        return add(total, [swap(part[1], 1), swap(pair, 2)], BF16)

    return local


def solution(mesh):
    return jax.shard_map(
        make_local(mesh.shape["wide"], mesh.shape["narrow"]),
        mesh=mesh,
        in_specs=(
            P(("groups", "wide"), "narrow"),
            P("narrow", "wide"),
            P("narrow", "wide"),
            P("wide", "narrow"),
        ),
        out_specs=P(("groups", "wide"), "narrow"),
        check_vma=False,
    )
```

```python
import functools

import jax
import jax.numpy as jnp
from jax import lax
from jax.experimental import pallas as pl
from jax.experimental.pallas import tpu as pltpu
from jax.sharding import PartitionSpec as P

F32 = jnp.float32
BF16 = jnp.bfloat16


def call(kernel, name, out_shape, flops, vmem, *operands):
    return pl.pallas_call(
        kernel,
        out_shape=out_shape,
        compiler_params=pltpu.CompilerParams(vmem_limit_bytes=vmem),
        cost_estimate=pl.CostEstimate(flops=flops, bytes_accessed=0, transcendentals=0),
        name=name,
    )(*operands)


def fetch_kernel(pieces, count, *refs):
    sems = refs[-1]
    copies = []
    for n in range(count):
        source, target = refs[n], refs[count + n]
        step = source.shape[0] // pieces
        for i in range(pieces):
            part = pl.ds(i * step, step)
            copies.append(pltpu.make_async_copy(source.at[part], target.at[part], sems.at[n, i]))
    for copy in copies:
        copy.start()
    for copy in copies:
        copy.wait()


def fetch(weights, pieces=4):
    count = len(weights)
    return pl.pallas_call(
        functools.partial(fetch_kernel, pieces, count),
        in_specs=[pl.BlockSpec(memory_space=pl.ANY)] * count,
        out_specs=[pl.BlockSpec(memory_space=pltpu.VMEM)] * count,
        out_shape=[jax.ShapeDtypeStruct(w.shape, w.dtype) for w in weights],
        scratch_shapes=[pltpu.SemaphoreType.DMA((count, pieces))],
        compiler_params=pltpu.CompilerParams(vmem_limit_bytes=43 << 20),
        cost_estimate=pl.CostEstimate(flops=4000000000, bytes_accessed=0, transcendentals=0),
        name="fetch",
    )(*weights)


def pack_kernel(*refs):
    *block_refs, out_ref = refs
    rows = block_refs[0].shape[0]
    for k, ref in enumerate(block_refs):
        out_ref[k * rows:(k + 1) * rows, :] = ref[...]


def pack(blocks):
    rows, width = blocks[0].shape
    out = jax.ShapeDtypeStruct((len(blocks) * rows, width), BF16)
    return call(pack_kernel, "pack", out, 4000000000, 2 << 20, *blocks)


def project_kernel(*refs):
    *block_refs, weight_ref, out_ref = refs
    rows = jnp.concatenate([ref[...] for ref in block_refs], axis=0)
    out_ref[...] = jnp.dot(rows, weight_ref[...], preferred_element_type=F32)


def project(blocks, weight):
    rows = sum(block.shape[0] for block in blocks)
    out = jax.ShapeDtypeStruct((rows, weight.shape[1]), F32)
    return call(project_kernel, "project", out, 400000000, 4 << 20, *blocks, weight)


def down_kernel(gate_ref, gate_other_ref, up_ref, up_other_ref, weight_ref, *out_refs):
    gate_sum = gate_ref[...] + gate_other_ref[...]
    up_sum = up_ref[...] + up_other_ref[...]
    hidden = (jax.nn.silu(gate_sum) * up_sum).astype(BF16)
    width = weight_ref.shape[1]
    tile = min(512, width)
    rows = out_refs[0].shape[0]

    def column_tile(step, carry):
        columns = pl.ds(pl.multiple_of(step * tile, tile), tile)
        partial = jnp.dot(hidden, weight_ref[:, columns], preferred_element_type=F32)
        for k, out_ref in enumerate(out_refs):
            out_ref[:, columns] = partial[k * rows:(k + 1) * rows].astype(out_ref.dtype)
        return carry

    lax.fori_loop(0, width // tile, column_tile, 0, unroll=True)


def down(gate, gate_other, up, up_other, weight, rows, dtypes):
    width = weight.shape[1]
    outs = [jax.ShapeDtypeStruct((rows, width), dtype) for dtype in dtypes]
    flops = 2 * gate.shape[0] * weight.shape[0] * width
    return call(
        down_kernel, "down", outs, flops, 4 << 20, gate, gate_other, up, up_other, weight
    )


def add_kernel(count, own_ref, *refs):
    total = own_ref[...]
    for ref in refs[:count]:
        total = total + ref[...].astype(F32)
    refs[-1][...] = total.astype(refs[-1].dtype)


def add(own, arrived, dtype, hint=1000000, after=()):
    count = len(arrived)
    return pl.pallas_call(
        functools.partial(add_kernel, count),
        in_specs=[pl.BlockSpec(memory_space=pltpu.VMEM)] * (1 + count)
        + [pl.BlockSpec(memory_space=pl.ANY)] * len(after),
        out_shape=jax.ShapeDtypeStruct(own.shape, dtype),
        compiler_params=pltpu.CompilerParams(vmem_limit_bytes=2 << 20),
        cost_estimate=pl.CostEstimate(flops=hint, bytes_accessed=0, transcendentals=0),
        name="add",
    )(own, *arrived, *after)


def make_local(wide, narrow):
    fars = list(range(4, wide, 4))

    def swap(value, bits):
        return lax.ppermute(value, "wide", [(i, i ^ bits) for i in range(wide)])

    def across_cores(value):
        return lax.ppermute(value, "narrow", [(i, (i + 1) % narrow) for i in range(narrow)])

    def local(tokens, gate_weight, up_weight, down_weight):
        rows = tokens.shape[0]
        block = {0: tokens}
        for far in fars:
            block[far] = swap(tokens, far)
        block[2] = swap(tokens, 2)
        block[1] = swap(tokens, 1)
        gate_held, up_held = fetch([gate_weight, up_weight])
        block[1], block[2], gate_held, up_held = lax.optimization_barrier(
            (block[1], block[2], gate_held, up_held)
        )
        block[3] = swap(block[2], 1)
        for far in fars:
            for near in (2, 3, 1):
                block[far + near] = swap(block[far], near)
        stay = [0, 2] + fars
        near_blocks = pack([block[b] for b in (0, 2, 1, 3)])
        order = [0, 2, 1, 3] + [far + near for far in fars for near in (0, 3, 2, 1)]
        far_blocks = [block[b] for b in order[4:]]
        gate_part = project([near_blocks] + far_blocks, gate_held)
        up_part = project([near_blocks] + far_blocks, up_held)
        outs = down(
            gate_part, across_cores(gate_part), up_part, across_cores(up_part),
            down_weight, rows, [F32 if b in stay else BF16 for b in order],
        )
        part = dict(zip(order, outs))
        sums = []
        for far in fars:
            quad = [swap(part[far + near], near) for near in (2, 3, 1)]
            sums.append(add(part[far], quad, BF16))
        arrived = [swap(value, far) for value, far in zip(sums, fars)]
        part[3], sums[0] = lax.optimization_barrier((part[3], sums[0]))
        pair = add(part[2], [swap(part[3], 1)], BF16)
        total = add(part[0], arrived, F32, 1500000000)
        return add(total, [swap(part[1], 1), swap(pair, 2)], BF16)

    return local


def solution(mesh):
    return jax.shard_map(
        make_local(mesh.shape["wide"], mesh.shape["narrow"]),
        mesh=mesh,
        in_specs=(
            P(("groups", "wide"), "narrow"),
            P("narrow", "wide"),
            P("narrow", "wide"),
            P("wide", "narrow"),
        ),
        out_specs=P(("groups", "wide"), "narrow"),
        check_vma=False,
    )
```

```python
import functools

import jax
import jax.numpy as jnp
from jax import lax
from jax.experimental import pallas as pl
from jax.experimental.pallas import tpu as pltpu
from jax.sharding import PartitionSpec as P

F32 = jnp.float32
BF16 = jnp.bfloat16


def call(kernel, name, out_shape, flops, vmem, *operands):
    return pl.pallas_call(
        kernel,
        out_shape=out_shape,
        compiler_params=pltpu.CompilerParams(vmem_limit_bytes=vmem),
        cost_estimate=pl.CostEstimate(flops=flops, bytes_accessed=0, transcendentals=0),
        name=name,
    )(*operands)


def fetch_kernel(pieces, count, *refs):
    sems = refs[-1]
    copies = []
    for n in range(count):
        source, target = refs[n], refs[count + n]
        step = source.shape[0] // pieces
        for i in range(pieces):
            part = pl.ds(i * step, step)
            copies.append(pltpu.make_async_copy(source.at[part], target.at[part], sems.at[n, i]))
    for copy in copies:
        copy.start()
    for copy in copies:
        copy.wait()


def fetch(weights, pieces=4):
    count = len(weights)
    return pl.pallas_call(
        functools.partial(fetch_kernel, pieces, count),
        in_specs=[pl.BlockSpec(memory_space=pl.ANY)] * count,
        out_specs=[pl.BlockSpec(memory_space=pltpu.VMEM)] * count,
        out_shape=[jax.ShapeDtypeStruct(w.shape, w.dtype) for w in weights],
        scratch_shapes=[pltpu.SemaphoreType.DMA((count, pieces))],
        compiler_params=pltpu.CompilerParams(vmem_limit_bytes=43 << 20),
        cost_estimate=pl.CostEstimate(flops=4000000000, bytes_accessed=0, transcendentals=0),
        name="fetch",
    )(*weights)


def pack_kernel(*refs):
    *block_refs, out_ref = refs
    rows = block_refs[0].shape[0]
    for k, ref in enumerate(block_refs):
        out_ref[k * rows:(k + 1) * rows, :] = ref[...]


def pack(blocks):
    rows, width = blocks[0].shape
    out = jax.ShapeDtypeStruct((len(blocks) * rows, width), BF16)
    return call(pack_kernel, "pack", out, 4000000000, 2 << 20, *blocks)


def project_kernel(*refs):
    *block_refs, weight_ref, out_ref = refs
    rows = jnp.concatenate([ref[...] for ref in block_refs], axis=0)
    out_ref[...] = jnp.dot(rows, weight_ref[...], preferred_element_type=F32)


def project(blocks, weight):
    rows = sum(block.shape[0] for block in blocks)
    out = jax.ShapeDtypeStruct((rows, weight.shape[1]), F32)
    return call(project_kernel, "project", out, 400000000, 4 << 20, *blocks, weight)


def down_kernel(gate_ref, gate_other_ref, up_ref, up_other_ref, weight_ref, *out_refs):
    gate_sum = gate_ref[...] + gate_other_ref[...]
    up_sum = up_ref[...] + up_other_ref[...]
    hidden = (jax.nn.silu(gate_sum) * up_sum).astype(BF16)
    width = weight_ref.shape[1]
    tile = min(512, width)
    rows = out_refs[0].shape[0]

    def column_tile(step, carry):
        columns = pl.ds(pl.multiple_of(step * tile, tile), tile)
        partial = jnp.dot(hidden, weight_ref[:, columns], preferred_element_type=F32)
        for k, out_ref in enumerate(out_refs):
            out_ref[:, columns] = partial[k * rows:(k + 1) * rows].astype(out_ref.dtype)
        return carry

    lax.fori_loop(0, width // tile, column_tile, 0, unroll=True)


def down(gate, gate_other, up, up_other, weight, rows, dtypes):
    width = weight.shape[1]
    outs = [jax.ShapeDtypeStruct((rows, width), dtype) for dtype in dtypes]
    flops = 2 * gate.shape[0] * weight.shape[0] * width
    return call(
        down_kernel, "down", outs, flops, 4 << 20, gate, gate_other, up, up_other, weight
    )


def add_kernel(count, own_ref, *refs):
    total = own_ref[...]
    for ref in refs[:count]:
        total = total + ref[...].astype(F32)
    refs[-1][...] = total.astype(refs[-1].dtype)


def add(own, arrived, dtype, hint=1000000, after=()):
    count = len(arrived)
    return pl.pallas_call(
        functools.partial(add_kernel, count),
        in_specs=[pl.BlockSpec(memory_space=pltpu.VMEM)] * (1 + count)
        + [pl.BlockSpec(memory_space=pl.ANY)] * len(after),
        out_shape=jax.ShapeDtypeStruct(own.shape, dtype),
        compiler_params=pltpu.CompilerParams(vmem_limit_bytes=2 << 20),
        cost_estimate=pl.CostEstimate(flops=hint, bytes_accessed=0, transcendentals=0),
        name="add",
    )(own, *arrived, *after)


def make_local(wide, narrow):
    fars = list(range(4, wide, 4))

    def swap(value, bits):
        return lax.ppermute(value, "wide", [(i, i ^ bits) for i in range(wide)])

    def across_cores(value):
        return lax.ppermute(value, "narrow", [(i, (i + 1) % narrow) for i in range(narrow)])

    def local(tokens, gate_weight, up_weight, down_weight):
        rows = tokens.shape[0]
        block = {0: tokens}
        for far in fars:
            block[far] = swap(tokens, far)
        block[2] = swap(tokens, 2)
        block[1] = swap(tokens, 1)
        gate_held, up_held = fetch([gate_weight, up_weight])
        block[1], block[2], gate_held, up_held = lax.optimization_barrier(
            (block[1], block[2], gate_held, up_held)
        )
        block[3] = swap(block[2], 1)
        for far in fars:
            for near in (2, 3, 1):
                block[far + near] = swap(block[far], near)
        stay = [0, 2] + fars
        near_blocks = pack([block[b] for b in (0, 2, 1, 3)])
        order = [0, 2, 1, 3] + [far + near for far in fars for near in (0, 3, 2, 1)]
        far_blocks = [block[b] for b in order[4:]]
        gate_part = project([near_blocks] + far_blocks, gate_held)
        up_part = project([near_blocks] + far_blocks, up_held)
        outs = down(
            gate_part, across_cores(gate_part), up_part, across_cores(up_part),
            down_weight, rows, [F32 if b in stay else BF16 for b in order],
        )
        part = dict(zip(order, outs))
        sums = []
        for far in fars:
            quad = [swap(part[far + near], near) for near in (2, 3, 1)]
            sums.append(add(part[far], quad, BF16))
        arrived = [swap(value, far) for value, far in zip(sums, fars)]
        pair = add(part[2], [swap(part[3], 1)], BF16, after=sums)
        total = add(part[0], arrived, F32, 1500000000)
        return add(total, [swap(part[1], 1), swap(pair, 2)], BF16)

    return local


def solution(mesh):
    return jax.shard_map(
        make_local(mesh.shape["wide"], mesh.shape["narrow"]),
        mesh=mesh,
        in_specs=(
            P(("groups", "wide"), "narrow"),
            P("narrow", "wide"),
            P("narrow", "wide"),
            P("wide", "narrow"),
        ),
        out_specs=P(("groups", "wide"), "narrow"),
        check_vma=False,
    )
```

```python
import functools

import jax
import jax.numpy as jnp
from jax import lax
from jax.experimental import pallas as pl
from jax.experimental.pallas import tpu as pltpu
from jax.sharding import PartitionSpec as P

F32 = jnp.float32
BF16 = jnp.bfloat16


def call(kernel, name, out_shape, flops, vmem, *operands):
    return pl.pallas_call(
        kernel,
        out_shape=out_shape,
        compiler_params=pltpu.CompilerParams(vmem_limit_bytes=vmem),
        cost_estimate=pl.CostEstimate(flops=flops, bytes_accessed=0, transcendentals=0),
        name=name,
    )(*operands)


def fetch_kernel(pieces, count, *refs):
    sems = refs[-1]
    copies = []
    for n in range(count):
        source, target = refs[n], refs[count + n]
        step = source.shape[0] // pieces
        for i in range(pieces):
            part = pl.ds(i * step, step)
            copies.append(pltpu.make_async_copy(source.at[part], target.at[part], sems.at[n, i]))
    for copy in copies:
        copy.start()
    for copy in copies:
        copy.wait()


def fetch(weights, pieces=4):
    count = len(weights)
    return pl.pallas_call(
        functools.partial(fetch_kernel, pieces, count),
        in_specs=[pl.BlockSpec(memory_space=pl.ANY)] * count,
        out_specs=[pl.BlockSpec(memory_space=pltpu.VMEM)] * count,
        out_shape=[jax.ShapeDtypeStruct(w.shape, w.dtype) for w in weights],
        scratch_shapes=[pltpu.SemaphoreType.DMA((count, pieces))],
        compiler_params=pltpu.CompilerParams(vmem_limit_bytes=43 << 20),
        cost_estimate=pl.CostEstimate(flops=4000000000, bytes_accessed=0, transcendentals=0),
        name="fetch",
    )(*weights)


def spread_kernel(count, block_ref, out_ref):
    rows = block_ref.shape[0]
    for k in range(count):
        out_ref[k * rows:(k + 1) * rows, :] = block_ref[...]


def spread(block, count):
    rows, width = block.shape
    out = jax.ShapeDtypeStruct((count * rows, width), BF16)
    return call(functools.partial(spread_kernel, count), "spread", out, 1000000, 2 << 20, block)


def project_kernel(*refs):
    *block_refs, weight_ref, out_ref = refs
    rows = jnp.concatenate([ref[...] for ref in block_refs], axis=0)
    out_ref[...] = jnp.dot(rows, weight_ref[...], preferred_element_type=F32)


def project(blocks, weight):
    rows = sum(block.shape[0] for block in blocks)
    out = jax.ShapeDtypeStruct((rows, weight.shape[1]), F32)
    return call(project_kernel, "project", out, 400000000, 4 << 20, *blocks, weight)


def down_kernel(gate_ref, gate_other_ref, up_ref, up_other_ref, weight_ref, *out_refs):
    gate_sum = gate_ref[...] + gate_other_ref[...]
    up_sum = up_ref[...] + up_other_ref[...]
    hidden = (jax.nn.silu(gate_sum) * up_sum).astype(BF16)
    width = weight_ref.shape[1]
    tile = min(512, width)
    rows = out_refs[0].shape[0]

    def column_tile(step, carry):
        columns = pl.ds(pl.multiple_of(step * tile, tile), tile)
        partial = jnp.dot(hidden, weight_ref[:, columns], preferred_element_type=F32)
        for k, out_ref in enumerate(out_refs):
            out_ref[:, columns] = partial[k * rows:(k + 1) * rows].astype(out_ref.dtype)
        return carry

    lax.fori_loop(0, width // tile, column_tile, 0, unroll=True)


def down(gate, gate_other, up, up_other, weight, rows, dtypes):
    width = weight.shape[1]
    outs = [jax.ShapeDtypeStruct((rows, width), dtype) for dtype in dtypes]
    flops = 2 * gate.shape[0] * weight.shape[0] * width
    return call(
        down_kernel, "down", outs, flops, 4 << 20, gate, gate_other, up, up_other, weight
    )


def add_kernel(own_ref, *refs):
    total = own_ref[...].astype(F32)
    for ref in refs[:-1]:
        total = total + ref[...].astype(F32)
    refs[-1][...] = total.astype(refs[-1].dtype)


def add(own, arrived, dtype, hint=1000000):
    out = jax.ShapeDtypeStruct(own.shape, dtype)
    return call(add_kernel, "add", out, hint, 2 << 20, own, *arrived)


def fold_kernel(count, chunks_ref, out_ref):
    rows = out_ref.shape[0]
    total = chunks_ref[:rows, :].astype(F32)
    for k in range(1, count):
        total = total + chunks_ref[k * rows:(k + 1) * rows, :].astype(F32)
    out_ref[...] = total.astype(out_ref.dtype)


def fold(chunks, count, dtype, hint=1000000):
    rows, width = chunks.shape
    out = jax.ShapeDtypeStruct((rows // count, width), dtype)
    return call(functools.partial(fold_kernel, count), "fold", out, hint, 2 << 20, chunks)


def make_local(wide, narrow):
    fars = list(range(4, wide, 4))
    quads = [list(range(first, first + 4)) for first in range(0, wide, 4)]

    def swap(value, bits):
        return lax.ppermute(value, "wide", [(i, i ^ bits) for i in range(wide)])

    def across_cores(value):
        return lax.ppermute(value, "narrow", [(i, (i + 1) % narrow) for i in range(narrow)])

    def in_quad(value):
        return lax.all_to_all(value, "wide", 0, 0, axis_index_groups=quads, tiled=True)

    def local(tokens, gate_weight, up_weight, down_weight):
        rows = tokens.shape[0]
        away = [swap(tokens, far) for far in fars]
        near = in_quad(spread(tokens, 4))
        gate_held, up_held = fetch([gate_weight, up_weight])
        groups = [near] + [in_quad(spread(value, 4)) for value in away]
        gate_part = project(groups, gate_held)
        up_part = project(groups, up_held)
        parts = down(
            gate_part, across_cores(gate_part), up_part, across_cores(up_part),
            down_weight, 4 * rows, [BF16] * len(groups),
        )
        sums = [fold(in_quad(part), 4, BF16) for part in parts[1:]]
        arrived = [swap(value, far) for value, far in zip(sums, fars)]
        total = fold(in_quad(parts[0]), 4, F32)
        return add(total, arrived, BF16)

    return local


def solution(mesh):
    return jax.shard_map(
        make_local(mesh.shape["wide"], mesh.shape["narrow"]),
        mesh=mesh,
        in_specs=(
            P(("groups", "wide"), "narrow"),
            P("narrow", "wide"),
            P("narrow", "wide"),
            P("wide", "narrow"),
        ),
        out_specs=P(("groups", "wide"), "narrow"),
        check_vma=False,
    )
```

```python
import functools

import jax
import jax.numpy as jnp
from jax import lax
from jax.experimental import pallas as pl
from jax.experimental.pallas import tpu as pltpu
from jax.sharding import PartitionSpec as P

F32 = jnp.float32
BF16 = jnp.bfloat16


def call(kernel, name, out_shape, hint, vmem, *operands, after=()):
    return pl.pallas_call(
        kernel,
        in_specs=[pl.BlockSpec(memory_space=pltpu.VMEM)] * len(operands)
        + [pl.BlockSpec(memory_space=pl.ANY)] * len(after),
        out_shape=out_shape,
        compiler_params=pltpu.CompilerParams(vmem_limit_bytes=vmem),
        cost_estimate=pl.CostEstimate(flops=hint, bytes_accessed=0, transcendentals=0),
        name=name,
    )(*operands, *after)


def fetch_kernel(pieces, count, *refs):
    sems = refs[-1]
    copies = []
    for n in range(count):
        source, target = refs[n], refs[count + n]
        step = source.shape[0] // pieces
        for i in range(pieces):
            part = pl.ds(i * step, step)
            copies.append(pltpu.make_async_copy(source.at[part], target.at[part], sems.at[n, i]))
    for copy in copies:
        copy.start()
    for copy in copies:
        copy.wait()


def fetch(weights, pieces=4):
    count = len(weights)
    return pl.pallas_call(
        functools.partial(fetch_kernel, pieces, count),
        in_specs=[pl.BlockSpec(memory_space=pl.ANY)] * count,
        out_specs=[pl.BlockSpec(memory_space=pltpu.VMEM)] * count,
        out_shape=[jax.ShapeDtypeStruct(w.shape, w.dtype) for w in weights],
        scratch_shapes=[pltpu.SemaphoreType.DMA((count, pieces))],
        compiler_params=pltpu.CompilerParams(vmem_limit_bytes=43 << 20),
        cost_estimate=pl.CostEstimate(flops=4000000000, bytes_accessed=0, transcendentals=0),
        name="fetch",
    )(*weights)


def project_kernel(*refs):
    *block_refs, weight_ref, out_ref = refs
    rows = jnp.concatenate([ref[...] for ref in block_refs], axis=0)
    out_ref[...] = jnp.dot(rows, weight_ref[...], preferred_element_type=F32)


def project(blocks, weight, hint):
    rows = sum(block.shape[0] for block in blocks)
    out = jax.ShapeDtypeStruct((rows, weight.shape[1]), F32)
    return call(project_kernel, "project", out, hint, 4 << 20, *blocks, weight)


def down_kernel(blocks, gate_ref, gate_other_ref, up_ref, up_other_ref, weight_ref, *refs):
    out_refs = refs[-blocks:]
    gate_sum = gate_ref[...] + gate_other_ref[...]
    up_sum = up_ref[...] + up_other_ref[...]
    hidden = (jax.nn.silu(gate_sum) * up_sum).astype(BF16)
    width = weight_ref.shape[1]
    tile = min(512, width)
    rows = out_refs[0].shape[0]

    def column_tile(step, carry):
        columns = pl.ds(pl.multiple_of(step * tile, tile), tile)
        partial = jnp.dot(hidden, weight_ref[:, columns], preferred_element_type=F32)
        for k, out_ref in enumerate(out_refs):
            out_ref[:, columns] = partial[k * rows:(k + 1) * rows].astype(out_ref.dtype)
        return carry

    lax.fori_loop(0, width // tile, column_tile, 0, unroll=True)


def down(gate, gate_other, up, up_other, weight, rows, dtypes, after):
    width = weight.shape[1]
    outs = [jax.ShapeDtypeStruct((rows, width), dtype) for dtype in dtypes]
    hint = 2 * gate.shape[0] * weight.shape[0] * width
    return call(
        functools.partial(down_kernel, len(outs)), "down", outs, hint, 4 << 20,
        gate, gate_other, up, up_other, weight, after=after,
    )


def add_kernel(count, own_ref, *refs):
    total = own_ref[...]
    for ref in refs[:count]:
        total = total + ref[...].astype(F32)
    refs[-1][...] = total.astype(refs[-1].dtype)


def add(own, arrived, dtype, hint=1000000, after=()):
    out = jax.ShapeDtypeStruct(own.shape, dtype)
    kernel = functools.partial(add_kernel, len(arrived))
    return call(kernel, "add", out, hint, 2 << 20, own, *arrived, after=after)


def make_local(wide, narrow):
    fars = list(range(4, wide, 4))

    def swap(value, bits):
        return lax.ppermute(value, "wide", [(i, i ^ bits) for i in range(wide)])

    def across_cores(value):
        return lax.ppermute(value, "narrow", [(i, (i + 1) % narrow) for i in range(narrow)])

    def local(tokens, gate_weight, up_weight, down_weight):
        rows = tokens.shape[0]
        block = {0: tokens}
        for far in fars:
            block[far] = swap(tokens, far)
        block[2] = swap(tokens, 2)
        block[1] = swap(tokens, 1)
        gate_held, up_held = fetch([gate_weight, up_weight])
        block[1], block[2], gate_held, up_held = lax.optimization_barrier(
            (block[1], block[2], gate_held, up_held)
        )
        block[3] = swap(block[2], 1)
        for far in fars:
            for near in (2, 3, 1):
                block[far + near] = swap(block[far], near)

        def partials(order, gate_held, up_held, hint, after=()):
            blocks = [block[b] for b in order]
            gate_part = project(blocks, gate_held, hint)
            up_part = project(blocks, up_held, hint)
            outs = down(
                gate_part, across_cores(gate_part), up_part, across_cores(up_part),
                down_weight, rows, [F32 if b in stay else BF16 for b in order], after,
            )
            return dict(zip(order, outs))

        stay = [0] + fars
        part = partials([0, 1, 2], gate_held, up_held, 100000000)
        gate_held, up_held, part[1] = lax.optimization_barrier((gate_held, up_held, part[1]))
        total = add(part[0], [swap(part[1], 1), swap(part[2], 2)], F32, 1000000000)
        late = [3] + [far + near for far in fars for near in (0, 3, 2, 1)]
        part.update(partials(late, gate_held, up_held, 400000000, [total]))
        sums = []
        for far in fars:
            quad = [swap(part[far + near], near) for near in (2, 3, 1)]
            sums.append(add(part[far], quad, BF16))
        arrived = [swap(value, far) for value, far in zip(sums, fars)]
        return add(total, [swap(part[3], 3)] + arrived, BF16)

    return local


def solution(mesh):
    return jax.shard_map(
        make_local(mesh.shape["wide"], mesh.shape["narrow"]),
        mesh=mesh,
        in_specs=(
            P(("groups", "wide"), "narrow"),
            P("narrow", "wide"),
            P("narrow", "wide"),
            P("wide", "narrow"),
        ),
        out_specs=P(("groups", "wide"), "narrow"),
        check_vma=False,
    )
```

```python
import functools

import jax
import jax.numpy as jnp
from jax import lax
from jax.experimental import pallas as pl
from jax.experimental.pallas import tpu as pltpu
from jax.sharding import PartitionSpec as P

F32 = jnp.float32
BF16 = jnp.bfloat16


def call(kernel, name, out_shape, hint, vmem, *operands, after=()):
    return pl.pallas_call(
        kernel,
        in_specs=[pl.BlockSpec(memory_space=pltpu.VMEM)] * len(operands)
        + [pl.BlockSpec(memory_space=pl.ANY)] * len(after),
        out_shape=out_shape,
        compiler_params=pltpu.CompilerParams(vmem_limit_bytes=vmem),
        cost_estimate=pl.CostEstimate(flops=hint, bytes_accessed=0, transcendentals=0),
        name=name,
    )(*operands, *after)


def fetch_kernel(pieces, count, *refs):
    sems = refs[-1]
    copies = []
    for n in range(count):
        source, target = refs[n], refs[count + n]
        step = source.shape[0] // pieces
        for i in range(pieces):
            part = pl.ds(i * step, step)
            copies.append(pltpu.make_async_copy(source.at[part], target.at[part], sems.at[n, i]))
    for copy in copies:
        copy.start()
    for copy in copies:
        copy.wait()


def fetch(weights, pieces=4):
    count = len(weights)
    return pl.pallas_call(
        functools.partial(fetch_kernel, pieces, count),
        in_specs=[pl.BlockSpec(memory_space=pl.ANY)] * count,
        out_specs=[pl.BlockSpec(memory_space=pltpu.VMEM)] * count,
        out_shape=[jax.ShapeDtypeStruct(w.shape, w.dtype) for w in weights],
        scratch_shapes=[pltpu.SemaphoreType.DMA((count, pieces))],
        compiler_params=pltpu.CompilerParams(vmem_limit_bytes=43 << 20),
        cost_estimate=pl.CostEstimate(flops=4000000000, bytes_accessed=0, transcendentals=0),
        name="fetch",
    )(*weights)


def project_kernel(*refs):
    *block_refs, weight_ref, out_ref = refs
    rows = jnp.concatenate([ref[...] for ref in block_refs], axis=0)
    out_ref[...] = jnp.dot(rows, weight_ref[...], preferred_element_type=F32)


def project(blocks, weight, hint):
    rows = sum(block.shape[0] for block in blocks)
    out = jax.ShapeDtypeStruct((rows, weight.shape[1]), F32)
    return call(project_kernel, "project", out, hint, 4 << 20, *blocks, weight)


def down_kernel(blocks, gate_ref, gate_other_ref, up_ref, up_other_ref, weight_ref, *refs):
    out_refs = refs[-blocks:]
    gate_sum = gate_ref[...] + gate_other_ref[...]
    up_sum = up_ref[...] + up_other_ref[...]
    hidden = (jax.nn.silu(gate_sum) * up_sum).astype(BF16)
    width = weight_ref.shape[1]
    tile = min(512, width)
    rows = out_refs[0].shape[0]

    def column_tile(step, carry):
        columns = pl.ds(pl.multiple_of(step * tile, tile), tile)
        partial = jnp.dot(hidden, weight_ref[:, columns], preferred_element_type=F32)
        for k, out_ref in enumerate(out_refs):
            out_ref[:, columns] = partial[k * rows:(k + 1) * rows].astype(out_ref.dtype)
        return carry

    lax.fori_loop(0, width // tile, column_tile, 0, unroll=True)


def down(gate, gate_other, up, up_other, weight, rows, dtypes, after):
    width = weight.shape[1]
    outs = [jax.ShapeDtypeStruct((rows, width), dtype) for dtype in dtypes]
    hint = 2 * gate.shape[0] * weight.shape[0] * width
    return call(
        functools.partial(down_kernel, len(outs)), "down", outs, hint, 4 << 20,
        gate, gate_other, up, up_other, weight, after=after,
    )


def add_kernel(count, own_ref, *refs):
    total = own_ref[...]
    for ref in refs[:count]:
        total = total + ref[...].astype(F32)
    refs[-1][...] = total.astype(refs[-1].dtype)


def add(own, arrived, dtype, hint=1000000, after=()):
    out = jax.ShapeDtypeStruct(own.shape, dtype)
    kernel = functools.partial(add_kernel, len(arrived))
    return call(kernel, "add", out, hint, 2 << 20, own, *arrived, after=after)


def make_local(wide, narrow):
    fars = list(range(4, wide, 4))

    def swap(value, bits):
        return lax.ppermute(value, "wide", [(i, i ^ bits) for i in range(wide)])

    def across_cores(value):
        return lax.ppermute(value, "narrow", [(i, (i + 1) % narrow) for i in range(narrow)])

    def local(tokens, gate_weight, up_weight, down_weight):
        rows = tokens.shape[0]
        block = {0: tokens}
        for far in fars:
            block[far] = swap(tokens, far)
        block[2] = swap(tokens, 2)
        block[1] = swap(tokens, 1)
        gate_held, up_held = fetch([gate_weight, up_weight])
        block[1], block[2], gate_held, up_held = lax.optimization_barrier(
            (block[1], block[2], gate_held, up_held)
        )
        block[3] = swap(block[2], 1)
        for far in fars:
            for near in (2, 3, 1):
                block[far + near] = swap(block[far], near)

        def partials(order, gate_held, up_held, hint, after=()):
            blocks = [block[b] for b in order]
            gate_part = project(blocks, gate_held, hint)
            up_part = project(blocks, up_held, hint)
            outs = down(
                gate_part, across_cores(gate_part), up_part, across_cores(up_part),
                down_weight, rows, [F32 if b in stay else BF16 for b in order], after,
            )
            return dict(zip(order, outs))

        stay = [0] + fars
        part = partials([0, 1, 2], gate_held, up_held, 2000000000)
        gate_held, up_held, part[1] = lax.optimization_barrier((gate_held, up_held, part[1]))
        total = add(part[0], [swap(part[1], 1), swap(part[2], 2)], F32, 3000000000)
        late = [3] + [far + near for far in fars for near in (0, 3, 2, 1)]
        part.update(partials(late, gate_held, up_held, 400000000))
        sums = []
        for far in fars:
            quad = [swap(part[far + near], near) for near in (2, 3, 1)]
            sums.append(add(part[far], quad, BF16, after=[total]))
        arrived = [swap(value, far) for value, far in zip(sums, fars)]
        part[3], sums[-1] = lax.optimization_barrier((part[3], sums[-1]))
        total = add(total, arrived, F32, 3000000000)
        return add(total, [swap(part[3], 3)], BF16)

    return local


def solution(mesh):
    return jax.shard_map(
        make_local(mesh.shape["wide"], mesh.shape["narrow"]),
        mesh=mesh,
        in_specs=(
            P(("groups", "wide"), "narrow"),
            P("narrow", "wide"),
            P("narrow", "wide"),
            P("wide", "narrow"),
        ),
        out_specs=P(("groups", "wide"), "narrow"),
        check_vma=False,
    )
```

```python
import functools

import jax
import jax.numpy as jnp
from jax import lax
from jax.experimental import pallas as pl
from jax.experimental.pallas import tpu as pltpu
from jax.sharding import PartitionSpec as P

F32 = jnp.float32
BF16 = jnp.bfloat16


def call(kernel, name, out_shape, flops, vmem, *operands):
    return pl.pallas_call(
        kernel,
        out_shape=out_shape,
        compiler_params=pltpu.CompilerParams(vmem_limit_bytes=vmem),
        cost_estimate=pl.CostEstimate(flops=flops, bytes_accessed=0, transcendentals=0),
        name=name,
    )(*operands)


def fetch_kernel(pieces, count, *refs):
    sems = refs[-1]
    copies = []
    for n in range(count):
        source, target = refs[n], refs[count + n]
        step = source.shape[0] // pieces
        for i in range(pieces):
            part = pl.ds(i * step, step)
            copies.append(pltpu.make_async_copy(source.at[part], target.at[part], sems.at[n, i]))
    for copy in copies:
        copy.start()
    for copy in copies:
        copy.wait()


def fetch(weights, pieces=4):
    count = len(weights)
    return pl.pallas_call(
        functools.partial(fetch_kernel, pieces, count),
        in_specs=[pl.BlockSpec(memory_space=pl.ANY)] * count,
        out_specs=[pl.BlockSpec(memory_space=pltpu.VMEM)] * count,
        out_shape=[jax.ShapeDtypeStruct(w.shape, w.dtype) for w in weights],
        scratch_shapes=[pltpu.SemaphoreType.DMA((count, pieces))],
        compiler_params=pltpu.CompilerParams(vmem_limit_bytes=43 << 20),
        cost_estimate=pl.CostEstimate(flops=4000000000, bytes_accessed=0, transcendentals=0),
        name="fetch",
    )(*weights)


def pack_kernel(*refs):
    *block_refs, out_ref = refs
    rows = block_refs[0].shape[0]
    for k, ref in enumerate(block_refs):
        out_ref[k * rows:(k + 1) * rows, :] = ref[...]


def pack(blocks):
    rows, width = blocks[0].shape
    out = jax.ShapeDtypeStruct((len(blocks) * rows, width), BF16)
    return call(pack_kernel, "pack", out, 4000000000, 2 << 20, *blocks)


def project_kernel(*refs):
    *block_refs, weight_ref, out_ref = refs
    rows = jnp.concatenate([ref[...] for ref in block_refs], axis=0)
    out_ref[...] = jnp.dot(rows, weight_ref[...], preferred_element_type=F32)


def project(blocks, weight):
    rows = sum(block.shape[0] for block in blocks)
    out = jax.ShapeDtypeStruct((rows, weight.shape[1]), F32)
    return call(project_kernel, "project", out, 400000000, 4 << 20, *blocks, weight)


def down_kernel(gate_ref, gate_other_ref, up_ref, up_other_ref, weight_ref, *out_refs):
    gate_sum = gate_ref[...] + gate_other_ref[...]
    up_sum = up_ref[...] + up_other_ref[...]
    hidden = (jax.nn.silu(gate_sum) * up_sum).astype(BF16)
    width = weight_ref.shape[1]
    tile = min(512, width)
    rows = out_refs[0].shape[0]

    def column_tile(step, carry):
        columns = pl.ds(pl.multiple_of(step * tile, tile), tile)
        partial = jnp.dot(hidden, weight_ref[:, columns], preferred_element_type=F32)
        for k, out_ref in enumerate(out_refs):
            out_ref[:, columns] = partial[k * rows:(k + 1) * rows].astype(out_ref.dtype)
        return carry

    lax.fori_loop(0, width // tile, column_tile, 0, unroll=True)


def down(gate, gate_other, up, up_other, weight, rows, dtypes):
    width = weight.shape[1]
    outs = [jax.ShapeDtypeStruct((rows, width), dtype) for dtype in dtypes]
    flops = 2 * gate.shape[0] * weight.shape[0] * width
    return call(
        down_kernel, "down", outs, flops, 4 << 20, gate, gate_other, up, up_other, weight
    )


def add_kernel(count, own_ref, *refs):
    total = own_ref[...]
    for ref in refs[:count]:
        total = total + ref[...].astype(F32)
    refs[-1][...] = total.astype(refs[-1].dtype)


def add(own, arrived, dtype, hint=1000000, after=()):
    count = len(arrived)
    return pl.pallas_call(
        functools.partial(add_kernel, count),
        in_specs=[pl.BlockSpec(memory_space=pltpu.VMEM)] * (1 + count)
        + [pl.BlockSpec(memory_space=pl.ANY)] * len(after),
        out_shape=jax.ShapeDtypeStruct(own.shape, dtype),
        compiler_params=pltpu.CompilerParams(vmem_limit_bytes=2 << 20),
        cost_estimate=pl.CostEstimate(flops=hint, bytes_accessed=0, transcendentals=0),
        name="add",
    )(own, *arrived, *after)


def make_local(wide, narrow):
    fars = list(range(4, wide, 4))

    def swap(value, bits):
        return lax.ppermute(value, "wide", [(i, i ^ bits) for i in range(wide)])

    def across_cores(value):
        return lax.ppermute(value, "narrow", [(i, (i + 1) % narrow) for i in range(narrow)])

    def local(tokens, gate_weight, up_weight, down_weight):
        rows = tokens.shape[0]
        block = {0: tokens}
        for far in fars:
            block[far] = swap(tokens, far)
        block[2] = swap(tokens, 2)
        block[1] = swap(tokens, 1)
        gate_held, up_held = fetch([gate_weight, up_weight])
        block[1], block[2], gate_held, up_held = lax.optimization_barrier(
            (block[1], block[2], gate_held, up_held)
        )
        block[3] = swap(block[2], 1)
        for far in fars:
            for near in (2, 3, 1):
                block[far + near] = swap(block[far], near)
        stay = [0, 2] + fars
        near_blocks = pack([block[b] for b in (0, 2, 1, 3)])
        order = [0, 2, 1, 3] + [far + near for far in fars for near in (0, 3, 2, 1)]
        far_blocks = [block[b] for b in order[4:]]
        gate_part = project([near_blocks] + far_blocks, gate_held)
        up_part = project([near_blocks] + far_blocks, up_held)
        outs = down(
            gate_part, across_cores(gate_part), up_part, across_cores(up_part),
            down_weight, rows, [F32 if b in stay else BF16 for b in order],
        )
        part = dict(zip(order, outs))
        sums = []
        for far in fars:
            quad = [swap(part[far + near], near) for near in (2, 3, 1)]
            sums.append(add(part[far], quad, BF16))
        arrived = [swap(value, far) for value, far in zip(sums, fars)]
        pair = add(part[2], [swap(part[3], 1)], BF16, after=sums)
        part[1], pair = lax.optimization_barrier((part[1], pair))
        total = add(part[0], arrived, F32, 1500000000)
        return add(total, [swap(pair, 2), swap(part[1], 1)], BF16)

    return local


def solution(mesh):
    return jax.shard_map(
        make_local(mesh.shape["wide"], mesh.shape["narrow"]),
        mesh=mesh,
        in_specs=(
            P(("groups", "wide"), "narrow"),
            P("narrow", "wide"),
            P("narrow", "wide"),
            P("wide", "narrow"),
        ),
        out_specs=P(("groups", "wide"), "narrow"),
        check_vma=False,
    )
```

```python
import functools

import jax
import jax.numpy as jnp
from jax import lax
from jax.experimental import pallas as pl
from jax.experimental.pallas import tpu as pltpu
from jax.sharding import PartitionSpec as P

F32 = jnp.float32
BF16 = jnp.bfloat16


def call(kernel, name, out_shape, flops, vmem, *operands):
    return pl.pallas_call(
        kernel,
        out_shape=out_shape,
        compiler_params=pltpu.CompilerParams(vmem_limit_bytes=vmem),
        cost_estimate=pl.CostEstimate(flops=flops, bytes_accessed=0, transcendentals=0),
        name=name,
    )(*operands)


def fetch_kernel(pieces, count, *refs):
    sems = refs[-1]
    copies = []
    for n in range(count):
        source, target = refs[n], refs[count + n]
        step = source.shape[0] // pieces
        for i in range(pieces):
            part = pl.ds(i * step, step)
            copies.append(pltpu.make_async_copy(source.at[part], target.at[part], sems.at[n, i]))
    for copy in copies:
        copy.start()
    for copy in copies:
        copy.wait()


def fetch(weights, pieces=4):
    count = len(weights)
    return pl.pallas_call(
        functools.partial(fetch_kernel, pieces, count),
        in_specs=[pl.BlockSpec(memory_space=pl.ANY)] * count,
        out_specs=[pl.BlockSpec(memory_space=pltpu.VMEM)] * count,
        out_shape=[jax.ShapeDtypeStruct(w.shape, w.dtype) for w in weights],
        scratch_shapes=[pltpu.SemaphoreType.DMA((count, pieces))],
        compiler_params=pltpu.CompilerParams(vmem_limit_bytes=43 << 20),
        cost_estimate=pl.CostEstimate(flops=4000000000, bytes_accessed=0, transcendentals=0),
        name="fetch",
    )(*weights)


def pack_kernel(*refs):
    *block_refs, out_ref = refs
    rows = block_refs[0].shape[0]
    for k, ref in enumerate(block_refs):
        out_ref[k * rows:(k + 1) * rows, :] = ref[...]


def pack(blocks):
    rows, width = blocks[0].shape
    out = jax.ShapeDtypeStruct((len(blocks) * rows, width), BF16)
    return call(pack_kernel, "pack", out, 4000000000, 2 << 20, *blocks)


def project_kernel(*refs):
    *block_refs, weight_ref, out_ref = refs
    rows = jnp.concatenate([ref[...] for ref in block_refs], axis=0)
    out_ref[...] = jnp.dot(rows, weight_ref[...], preferred_element_type=F32)


def project(blocks, weight):
    rows = sum(block.shape[0] for block in blocks)
    out = jax.ShapeDtypeStruct((rows, weight.shape[1]), F32)
    return call(project_kernel, "project", out, 400000000, 4 << 20, *blocks, weight)


def down_kernel(gate_ref, gate_other_ref, up_ref, up_other_ref, weight_ref, *out_refs):
    gate_sum = gate_ref[...] + gate_other_ref[...]
    up_sum = up_ref[...] + up_other_ref[...]
    hidden = (jax.nn.silu(gate_sum) * up_sum).astype(BF16)
    width = weight_ref.shape[1]
    tile = min(512, width)
    rows = out_refs[0].shape[0]

    def column_tile(step, carry):
        columns = pl.ds(pl.multiple_of(step * tile, tile), tile)
        partial = jnp.dot(hidden, weight_ref[:, columns], preferred_element_type=F32)
        for k, out_ref in enumerate(out_refs):
            out_ref[:, columns] = partial[k * rows:(k + 1) * rows].astype(out_ref.dtype)
        return carry

    lax.fori_loop(0, width // tile, column_tile, 0, unroll=True)


def down(gate, gate_other, up, up_other, weight, rows, dtypes):
    width = weight.shape[1]
    outs = [jax.ShapeDtypeStruct((rows, width), dtype) for dtype in dtypes]
    flops = 2 * gate.shape[0] * weight.shape[0] * width
    return call(
        down_kernel, "down", outs, flops, 4 << 20, gate, gate_other, up, up_other, weight
    )


def add_kernel(count, own_ref, *refs):
    total = own_ref[...]
    for ref in refs[:count]:
        total = total + ref[...].astype(F32)
    refs[-1][...] = total.astype(refs[-1].dtype)


def add(own, arrived, dtype, hint=1000000, after=()):
    count = len(arrived)
    return pl.pallas_call(
        functools.partial(add_kernel, count),
        in_specs=[pl.BlockSpec(memory_space=pltpu.VMEM)] * (1 + count)
        + [pl.BlockSpec(memory_space=pl.ANY)] * len(after),
        out_shape=jax.ShapeDtypeStruct(own.shape, dtype),
        compiler_params=pltpu.CompilerParams(vmem_limit_bytes=2 << 20),
        cost_estimate=pl.CostEstimate(flops=hint, bytes_accessed=0, transcendentals=0),
        name="add",
    )(own, *arrived, *after)


def make_local(wide, narrow):
    fars = list(range(4, wide, 4))

    def swap(value, bits):
        return lax.ppermute(value, "wide", [(i, i ^ bits) for i in range(wide)])

    def across_cores(value):
        return lax.ppermute(value, "narrow", [(i, (i + 1) % narrow) for i in range(narrow)])

    def local(tokens, gate_weight, up_weight, down_weight):
        rows = tokens.shape[0]
        block = {0: tokens}
        for far in fars:
            block[far] = swap(tokens, far)
        block[2] = swap(tokens, 2)
        block[1] = swap(tokens, 1)
        gate_held, up_held = fetch([gate_weight, up_weight])
        block[1], block[2], gate_held, up_held = lax.optimization_barrier(
            (block[1], block[2], gate_held, up_held)
        )
        block[3] = swap(block[2], 1)
        for far in fars:
            for near in (2, 3, 1):
                block[far + near] = swap(block[far], near)
        stay = [0] + fars
        near_blocks = pack([block[b] for b in (0, 2, 1, 3)])
        order = [0, 2, 1, 3] + [far + near for far in fars for near in (0, 3, 2, 1)]
        far_blocks = [block[b] for b in order[4:]]
        gate_part = project([near_blocks] + far_blocks, gate_held)
        up_part = project([near_blocks] + far_blocks, up_held)
        outs = down(
            gate_part, across_cores(gate_part), up_part, across_cores(up_part),
            down_weight, rows, [F32 if b in stay else BF16 for b in order],
        )
        part = dict(zip(order, outs))
        sums = []
        for far in fars:
            quad = [swap(part[far + near], near) for near in (2, 3, 1)]
            sums.append(add(part[far], quad, BF16))
        arrived = [swap(value, far) for value, far in zip(sums, fars)]
        part[1], part[3], sums[0] = lax.optimization_barrier((part[1], part[3], sums[0]))
        total = add(part[0], [swap(part[2], 2)] + arrived, F32, 1500000000)
        return add(total, [swap(part[3], 3), swap(part[1], 1)], BF16)

    return local


def solution(mesh):
    return jax.shard_map(
        make_local(mesh.shape["wide"], mesh.shape["narrow"]),
        mesh=mesh,
        in_specs=(
            P(("groups", "wide"), "narrow"),
            P("narrow", "wide"),
            P("narrow", "wide"),
            P("wide", "narrow"),
        ),
        out_specs=P(("groups", "wide"), "narrow"),
        check_vma=False,
    )
```

```python
import functools

import jax
import jax.numpy as jnp
from jax import lax
from jax.experimental import pallas as pl
from jax.experimental.pallas import tpu as pltpu
from jax.sharding import PartitionSpec as P

F32 = jnp.float32
BF16 = jnp.bfloat16


def call(kernel, name, out_shape, flops, vmem, *operands):
    return pl.pallas_call(
        kernel,
        out_shape=out_shape,
        compiler_params=pltpu.CompilerParams(vmem_limit_bytes=vmem),
        cost_estimate=pl.CostEstimate(flops=flops, bytes_accessed=0, transcendentals=0),
        name=name,
    )(*operands)


def fetch_kernel(pieces, count, *refs):
    sems = refs[-1]
    copies = []
    for n in range(count):
        source, target = refs[n], refs[count + n]
        step = source.shape[0] // pieces
        for i in range(pieces):
            part = pl.ds(i * step, step)
            copies.append(pltpu.make_async_copy(source.at[part], target.at[part], sems.at[n, i]))
    for copy in copies:
        copy.start()
    for copy in copies:
        copy.wait()


def fetch(weights, pieces=4):
    count = len(weights)
    return pl.pallas_call(
        functools.partial(fetch_kernel, pieces, count),
        in_specs=[pl.BlockSpec(memory_space=pl.ANY)] * count,
        out_specs=[pl.BlockSpec(memory_space=pltpu.VMEM)] * count,
        out_shape=[jax.ShapeDtypeStruct(w.shape, w.dtype) for w in weights],
        scratch_shapes=[pltpu.SemaphoreType.DMA((count, pieces))],
        compiler_params=pltpu.CompilerParams(vmem_limit_bytes=43 << 20),
        cost_estimate=pl.CostEstimate(flops=4000000000, bytes_accessed=0, transcendentals=0),
        name="fetch",
    )(*weights)


def project_kernel(*refs):
    *block_refs, weight_ref, out_ref = refs
    rows = jnp.concatenate([ref[...] for ref in block_refs], axis=0)
    out_ref[...] = jnp.dot(rows, weight_ref[...], preferred_element_type=F32)


def project(blocks, weight):
    rows = sum(block.shape[0] for block in blocks)
    out = jax.ShapeDtypeStruct((rows, weight.shape[1]), F32)
    return call(project_kernel, "project", out, 400000000, 4 << 20, *blocks, weight)


def down_kernel(gate_ref, gate_other_ref, up_ref, up_other_ref, weight_ref, *out_refs):
    gate_sum = gate_ref[...] + gate_other_ref[...]
    up_sum = up_ref[...] + up_other_ref[...]
    hidden = (jax.nn.silu(gate_sum) * up_sum).astype(BF16)
    width = weight_ref.shape[1]
    tile = min(512, width)
    rows = out_refs[0].shape[0]

    def column_tile(step, carry):
        columns = pl.ds(pl.multiple_of(step * tile, tile), tile)
        partial = jnp.dot(hidden, weight_ref[:, columns], preferred_element_type=F32)
        for k, out_ref in enumerate(out_refs):
            out_ref[:, columns] = partial[k * rows:(k + 1) * rows].astype(out_ref.dtype)
        return carry

    lax.fori_loop(0, width // tile, column_tile, 0, unroll=True)


def down(gate, gate_other, up, up_other, weight, rows, dtypes):
    width = weight.shape[1]
    outs = [jax.ShapeDtypeStruct((rows, width), dtype) for dtype in dtypes]
    flops = 2 * gate.shape[0] * weight.shape[0] * width
    return call(
        down_kernel, "down", outs, flops, 4 << 20, gate, gate_other, up, up_other, weight
    )


def add_kernel(count, own_ref, *refs):
    total = own_ref[...]
    for ref in refs[:count]:
        total = total + ref[...].astype(F32)
    refs[-1][...] = total.astype(refs[-1].dtype)


def add(own, arrived, dtype, hint=1000000, after=()):
    count = len(arrived)
    return pl.pallas_call(
        functools.partial(add_kernel, count),
        in_specs=[pl.BlockSpec(memory_space=pltpu.VMEM)] * (1 + count)
        + [pl.BlockSpec(memory_space=pl.ANY)] * len(after),
        out_shape=jax.ShapeDtypeStruct(own.shape, dtype),
        compiler_params=pltpu.CompilerParams(vmem_limit_bytes=2 << 20),
        cost_estimate=pl.CostEstimate(flops=hint, bytes_accessed=0, transcendentals=0),
        name="add",
    )(own, *arrived, *after)


def make_local(wide, narrow):
    fars = list(range(4, wide, 4))

    def swap(value, bits):
        return lax.ppermute(value, "wide", [(i, i ^ bits) for i in range(wide)])

    def across_cores(value):
        return lax.ppermute(value, "narrow", [(i, (i + 1) % narrow) for i in range(narrow)])

    def local(tokens, gate_weight, up_weight, down_weight):
        rows = tokens.shape[0]
        block = {0: tokens}
        for far in fars:
            block[far] = swap(tokens, far)
        block[2] = swap(tokens, 2)
        block[1] = swap(tokens, 1)
        gate_held, up_held = fetch([gate_weight, up_weight])
        first = [1, 2] + fars
        *hops, gate_held, up_held = lax.optimization_barrier(
            [block[b] for b in first] + [gate_held, up_held]
        )
        block.update(zip(first, hops))
        block[3] = swap(block[2], 1)
        for far in fars:
            for near in (2, 3, 1):
                block[far + near] = swap(block[far], near)
        stay = [0, 2] + fars
        order = list(range(wide))
        blocks = [block[b] for b in order]
        gate_part = project(blocks, gate_held)
        up_part = project(blocks, up_held)
        outs = down(
            gate_part, across_cores(gate_part), up_part, across_cores(up_part),
            down_weight, rows, [F32 if b in stay else BF16 for b in order],
        )
        part = dict(zip(order, outs))
        sums = []
        for far in fars:
            quad = [swap(part[far + near], near) for near in (2, 3, 1)]
            sums.append(add(part[far], quad, BF16))
        arrived = [swap(value, far) for value, far in zip(sums, fars)]
        pair = add(part[2], [swap(part[3], 1)], BF16, after=sums)
        part[1], pair = lax.optimization_barrier((part[1], pair))
        total = add(part[0], arrived, F32, 1500000000)
        return add(total, [swap(pair, 2), swap(part[1], 1)], BF16)

    return local


def solution(mesh):
    return jax.shard_map(
        make_local(mesh.shape["wide"], mesh.shape["narrow"]),
        mesh=mesh,
        in_specs=(
            P(("groups", "wide"), "narrow"),
            P("narrow", "wide"),
            P("narrow", "wide"),
            P("wide", "narrow"),
        ),
        out_specs=P(("groups", "wide"), "narrow"),
        check_vma=False,
    )
```

```python
import functools

import jax
import jax.numpy as jnp
from jax import lax
from jax.experimental import pallas as pl
from jax.experimental.pallas import tpu as pltpu
from jax.sharding import PartitionSpec as P

F32 = jnp.float32
BF16 = jnp.bfloat16


def call(kernel, name, out_shape, flops, vmem, *operands):
    return pl.pallas_call(
        kernel,
        out_shape=out_shape,
        compiler_params=pltpu.CompilerParams(vmem_limit_bytes=vmem),
        cost_estimate=pl.CostEstimate(flops=flops, bytes_accessed=0, transcendentals=0),
        name=name,
    )(*operands)


def fetch_kernel(pieces, count, *refs):
    sems = refs[-1]
    copies = []
    for n in range(count):
        source, target = refs[n], refs[count + n]
        step = source.shape[0] // pieces
        for i in range(pieces):
            part = pl.ds(i * step, step)
            copies.append(pltpu.make_async_copy(source.at[part], target.at[part], sems.at[n, i]))
    for copy in copies:
        copy.start()
    for copy in copies:
        copy.wait()


def fetch(weights, pieces=4):
    count = len(weights)
    return pl.pallas_call(
        functools.partial(fetch_kernel, pieces, count),
        in_specs=[pl.BlockSpec(memory_space=pl.ANY)] * count,
        out_specs=[pl.BlockSpec(memory_space=pltpu.VMEM)] * count,
        out_shape=[jax.ShapeDtypeStruct(w.shape, w.dtype) for w in weights],
        scratch_shapes=[pltpu.SemaphoreType.DMA((count, pieces))],
        compiler_params=pltpu.CompilerParams(vmem_limit_bytes=43 << 20),
        cost_estimate=pl.CostEstimate(flops=4000000000, bytes_accessed=0, transcendentals=0),
        name="fetch",
    )(*weights)


def project_kernel(*refs):
    *block_refs, weight_ref, out_ref = refs
    rows = jnp.concatenate([ref[...] for ref in block_refs], axis=0)
    out_ref[...] = jnp.dot(rows, weight_ref[...], preferred_element_type=F32)


def project(blocks, weight):
    rows = sum(block.shape[0] for block in blocks)
    out = jax.ShapeDtypeStruct((rows, weight.shape[1]), F32)
    return call(project_kernel, "project", out, 400000000, 4 << 20, *blocks, weight)


def down_kernel(gate_ref, gate_other_ref, up_ref, up_other_ref, weight_ref, *out_refs):
    gate_sum = gate_ref[...] + gate_other_ref[...]
    up_sum = up_ref[...] + up_other_ref[...]
    hidden = (jax.nn.silu(gate_sum) * up_sum).astype(BF16)
    width = weight_ref.shape[1]
    tile = min(512, width)
    rows = out_refs[0].shape[0]

    def column_tile(step, carry):
        columns = pl.ds(pl.multiple_of(step * tile, tile), tile)
        partial = jnp.dot(hidden, weight_ref[:, columns], preferred_element_type=F32)
        for k, out_ref in enumerate(out_refs):
            out_ref[:, columns] = partial[k * rows:(k + 1) * rows].astype(out_ref.dtype)
        return carry

    lax.fori_loop(0, width // tile, column_tile, 0, unroll=True)


def down(gate, gate_other, up, up_other, weight, rows, dtypes):
    width = weight.shape[1]
    outs = [jax.ShapeDtypeStruct((rows, width), dtype) for dtype in dtypes]
    flops = 2 * gate.shape[0] * weight.shape[0] * width
    return call(
        down_kernel, "down", outs, flops, 4 << 20, gate, gate_other, up, up_other, weight
    )


def add_kernel(count, own_ref, *refs):
    total = own_ref[...]
    for ref in refs[:count]:
        total = total + ref[...].astype(F32)
    refs[-1][...] = total.astype(refs[-1].dtype)


def add(own, arrived, dtype, hint=1000000, after=()):
    count = len(arrived)
    return pl.pallas_call(
        functools.partial(add_kernel, count),
        in_specs=[pl.BlockSpec(memory_space=pltpu.VMEM)] * (1 + count)
        + [pl.BlockSpec(memory_space=pl.ANY)] * len(after),
        out_shape=jax.ShapeDtypeStruct(own.shape, dtype),
        compiler_params=pltpu.CompilerParams(vmem_limit_bytes=2 << 20),
        cost_estimate=pl.CostEstimate(flops=hint, bytes_accessed=0, transcendentals=0),
        name="add",
    )(own, *arrived, *after)


def make_local(wide, narrow):
    fars = list(range(4, wide, 4))

    def swap(value, bits):
        return lax.ppermute(value, "wide", [(i, i ^ bits) for i in range(wide)])

    def across_cores(value):
        return lax.ppermute(value, "narrow", [(i, (i + 1) % narrow) for i in range(narrow)])

    def local(tokens, gate_weight, up_weight, down_weight):
        rows = tokens.shape[0]
        block = {0: tokens}
        for far in fars:
            block[far] = swap(tokens, far)
        for near in (1, 2, 3):
            block[near] = swap(tokens, near)
        gate_held, up_held = fetch([gate_weight, up_weight])
        *crossed, gate_held, up_held = lax.optimization_barrier(
            [block[far] for far in fars] + [gate_held, up_held]
        )
        block.update(zip(fars, crossed))
        for far in fars:
            for near in (2, 3, 1):
                block[far + near] = swap(block[far], near)
        stay = [0, 2] + fars
        order = [0, 3, 1, 2] + [far + near for far in fars for near in (0, 2, 1, 3)]
        blocks = [block[b] for b in order]
        gate_part = project(blocks, gate_held)
        up_part = project(blocks, up_held)
        outs = down(
            gate_part, across_cores(gate_part), up_part, across_cores(up_part),
            down_weight, rows, [F32 if b in stay else BF16 for b in order],
        )
        part = dict(zip(order, outs))
        sums = []
        for far in fars:
            quad = [swap(part[far + near], near) for near in (3, 1, 2)]
            sums.append(add(part[far], quad, BF16))
        arrived = [swap(value, far) for value, far in zip(sums, fars)]
        pair = add(part[2], [swap(part[3], 1)], BF16, after=sums)
        part[1], pair = lax.optimization_barrier((part[1], pair))
        total = add(part[0], arrived, F32, 1500000000)
        return add(total, [swap(pair, 2), swap(part[1], 1)], BF16)

    return local


def solution(mesh):
    return jax.shard_map(
        make_local(mesh.shape["wide"], mesh.shape["narrow"]),
        mesh=mesh,
        in_specs=(
            P(("groups", "wide"), "narrow"),
            P("narrow", "wide"),
            P("narrow", "wide"),
            P("wide", "narrow"),
        ),
        out_specs=P(("groups", "wide"), "narrow"),
        check_vma=False,
    )
```

```python
import functools

import jax
import jax.numpy as jnp
from jax import lax
from jax.experimental import pallas as pl
from jax.experimental.pallas import tpu as pltpu
from jax.sharding import PartitionSpec as P

F32 = jnp.float32
BF16 = jnp.bfloat16


def call(kernel, name, out_shape, flops, vmem, *operands):
    return pl.pallas_call(
        kernel,
        out_shape=out_shape,
        compiler_params=pltpu.CompilerParams(vmem_limit_bytes=vmem),
        cost_estimate=pl.CostEstimate(flops=flops, bytes_accessed=0, transcendentals=0),
        name=name,
    )(*operands)


def fetch_kernel(pieces, count, *refs):
    sems = refs[-1]
    copies = []
    for n in range(count):
        source, target = refs[n], refs[count + n]
        step = source.shape[0] // pieces
        for i in range(pieces):
            part = pl.ds(i * step, step)
            copies.append(pltpu.make_async_copy(source.at[part], target.at[part], sems.at[n, i]))
    for copy in copies:
        copy.start()
    for copy in copies:
        copy.wait()


def fetch(weights, pieces=4):
    count = len(weights)
    return pl.pallas_call(
        functools.partial(fetch_kernel, pieces, count),
        in_specs=[pl.BlockSpec(memory_space=pl.ANY)] * count,
        out_specs=[pl.BlockSpec(memory_space=pltpu.VMEM)] * count,
        out_shape=[jax.ShapeDtypeStruct(w.shape, w.dtype) for w in weights],
        scratch_shapes=[pltpu.SemaphoreType.DMA((count, pieces))],
        compiler_params=pltpu.CompilerParams(vmem_limit_bytes=43 << 20),
        cost_estimate=pl.CostEstimate(flops=4000000000, bytes_accessed=0, transcendentals=0),
        name="fetch",
    )(*weights)


def project_kernel(*refs):
    *block_refs, weight_ref, out_ref, sent_ref = refs
    rows = jnp.concatenate([ref[...] for ref in block_refs], axis=0)
    partial = jnp.dot(rows, weight_ref[...], preferred_element_type=F32)
    out_ref[...] = partial
    sent_ref[...] = partial.astype(BF16)


def project(blocks, weight):
    shape = (sum(block.shape[0] for block in blocks), weight.shape[1])
    outs = [jax.ShapeDtypeStruct(shape, F32), jax.ShapeDtypeStruct(shape, BF16)]
    return call(project_kernel, "project", outs, 400000000, 4 << 20, *blocks, weight)


def down_kernel(gate_ref, gate_other_ref, up_ref, up_other_ref, weight_ref, *out_refs):
    gate_sum = gate_ref[...] + gate_other_ref[...].astype(F32)
    up_sum = up_ref[...] + up_other_ref[...].astype(F32)
    hidden = (jax.nn.silu(gate_sum) * up_sum).astype(BF16)
    width = weight_ref.shape[1]
    tile = min(512, width)
    rows = out_refs[0].shape[0]

    def column_tile(step, carry):
        columns = pl.ds(pl.multiple_of(step * tile, tile), tile)
        partial = jnp.dot(hidden, weight_ref[:, columns], preferred_element_type=F32)
        for k, out_ref in enumerate(out_refs):
            out_ref[:, columns] = partial[k * rows:(k + 1) * rows].astype(out_ref.dtype)
        return carry

    lax.fori_loop(0, width // tile, column_tile, 0, unroll=True)


def down(gate, gate_other, up, up_other, weight, rows, dtypes):
    width = weight.shape[1]
    outs = [jax.ShapeDtypeStruct((rows, width), dtype) for dtype in dtypes]
    flops = 2 * gate.shape[0] * weight.shape[0] * width
    return call(
        down_kernel, "down", outs, flops, 4 << 20, gate, gate_other, up, up_other, weight
    )


def add_kernel(count, own_ref, *refs):
    total = own_ref[...]
    for ref in refs[:count]:
        total = total + ref[...].astype(F32)
    refs[-1][...] = total.astype(refs[-1].dtype)


def add(own, arrived, dtype, hint=1000000, after=()):
    count = len(arrived)
    return pl.pallas_call(
        functools.partial(add_kernel, count),
        in_specs=[pl.BlockSpec(memory_space=pltpu.VMEM)] * (1 + count)
        + [pl.BlockSpec(memory_space=pl.ANY)] * len(after),
        out_shape=jax.ShapeDtypeStruct(own.shape, dtype),
        compiler_params=pltpu.CompilerParams(vmem_limit_bytes=2 << 20),
        cost_estimate=pl.CostEstimate(flops=hint, bytes_accessed=0, transcendentals=0),
        name="add",
    )(own, *arrived, *after)


def make_local(wide, narrow):
    fars = list(range(4, wide, 4))

    def swap(value, bits):
        return lax.ppermute(value, "wide", [(i, i ^ bits) for i in range(wide)])

    def across_cores(value):
        return lax.ppermute(value, "narrow", [(i, (i + 1) % narrow) for i in range(narrow)])

    def local(tokens, gate_weight, up_weight, down_weight):
        rows = tokens.shape[0]
        block = {0: tokens}
        for far in fars:
            block[far] = swap(tokens, far)
        for near in (1, 2, 3):
            block[near] = swap(tokens, near)
        gate_held, up_held = fetch([gate_weight, up_weight])
        *crossed, gate_held, up_held = lax.optimization_barrier(
            [block[far] for far in fars] + [gate_held, up_held]
        )
        block.update(zip(fars, crossed))
        for far in fars:
            for near in (2, 3, 1):
                block[far + near] = swap(block[far], near)
        stay = [0, 2] + fars
        order = [0, 3, 1, 2] + [far + near for far in fars for near in (0, 2, 1, 3)]
        blocks = [block[b] for b in order]
        gate_part, gate_sent = project(blocks, gate_held)
        up_part, up_sent = project(blocks, up_held)
        outs = down(
            gate_part, across_cores(gate_sent), up_part, across_cores(up_sent),
            down_weight, rows, [F32 if b in stay else BF16 for b in order],
        )
        part = dict(zip(order, outs))
        sums = []
        for far in fars:
            quad = [swap(part[far + near], near) for near in (3, 1, 2)]
            sums.append(add(part[far], quad, BF16))
        arrived = [swap(value, far) for value, far in zip(sums, fars)]
        pair = add(part[2], [swap(part[3], 1)], BF16, after=sums)
        part[1], pair = lax.optimization_barrier((part[1], pair))
        total = add(part[0], arrived, F32, 1500000000)
        return add(total, [swap(pair, 2), swap(part[1], 1)], BF16)

    return local


def solution(mesh):
    return jax.shard_map(
        make_local(mesh.shape["wide"], mesh.shape["narrow"]),
        mesh=mesh,
        in_specs=(
            P(("groups", "wide"), "narrow"),
            P("narrow", "wide"),
            P("narrow", "wide"),
            P("wide", "narrow"),
        ),
        out_specs=P(("groups", "wide"), "narrow"),
        check_vma=False,
    )
```

```python
import functools

import jax
import jax.numpy as jnp
from jax import lax
from jax.experimental import pallas as pl
from jax.experimental.pallas import tpu as pltpu
from jax.sharding import PartitionSpec as P

F32 = jnp.float32
BF16 = jnp.bfloat16


def call(kernel, name, out_shape, flops, vmem, *operands):
    return pl.pallas_call(
        kernel,
        out_shape=out_shape,
        compiler_params=pltpu.CompilerParams(vmem_limit_bytes=vmem),
        cost_estimate=pl.CostEstimate(flops=flops, bytes_accessed=0, transcendentals=0),
        name=name,
    )(*operands)


def fetch_kernel(pieces, count, *refs):
    sems = refs[-1]
    copies = []
    for n in range(count):
        source, target = refs[n], refs[count + n]
        step = source.shape[0] // pieces
        for i in range(pieces):
            part = pl.ds(i * step, step)
            copies.append(pltpu.make_async_copy(source.at[part], target.at[part], sems.at[n, i]))
    for copy in copies:
        copy.start()
    for copy in copies:
        copy.wait()


def fetch(weights, pieces=4):
    count = len(weights)
    return pl.pallas_call(
        functools.partial(fetch_kernel, pieces, count),
        in_specs=[pl.BlockSpec(memory_space=pl.ANY)] * count,
        out_specs=[pl.BlockSpec(memory_space=pltpu.VMEM)] * count,
        out_shape=[jax.ShapeDtypeStruct(w.shape, w.dtype) for w in weights],
        scratch_shapes=[pltpu.SemaphoreType.DMA((count, pieces))],
        compiler_params=pltpu.CompilerParams(vmem_limit_bytes=43 << 20),
        cost_estimate=pl.CostEstimate(flops=4000000000, bytes_accessed=0, transcendentals=0),
        name="fetch",
    )(*weights)


def project_kernel(*refs):
    *block_refs, weight_ref, out_ref = refs
    rows = jnp.concatenate([ref[...] for ref in block_refs], axis=0)
    out_ref[...] = jnp.dot(rows, weight_ref[...], preferred_element_type=F32)


def project(blocks, weight):
    rows = sum(block.shape[0] for block in blocks)
    out = jax.ShapeDtypeStruct((rows, weight.shape[1]), F32)
    return call(project_kernel, "project", out, 400000000, 4 << 20, *blocks, weight)


def down_kernel(gate_ref, gate_other_ref, up_ref, up_other_ref, weight_ref, *out_refs):
    gate_sum = gate_ref[...] + gate_other_ref[...]
    up_sum = up_ref[...] + up_other_ref[...]
    hidden = (jax.nn.silu(gate_sum) * up_sum).astype(BF16)
    width = weight_ref.shape[1]
    tile = min(512, width)
    rows = out_refs[0].shape[0]

    def column_tile(step, carry):
        columns = pl.ds(pl.multiple_of(step * tile, tile), tile)
        partial = jnp.dot(hidden, weight_ref[:, columns], preferred_element_type=F32)
        for k, out_ref in enumerate(out_refs):
            out_ref[:, columns] = partial[k * rows:(k + 1) * rows].astype(out_ref.dtype)
        return carry

    lax.fori_loop(0, width // tile, column_tile, 0, unroll=True)


def down(gate, gate_other, up, up_other, weight, rows, dtypes):
    width = weight.shape[1]
    outs = [jax.ShapeDtypeStruct((rows, width), dtype) for dtype in dtypes]
    flops = 2 * gate.shape[0] * weight.shape[0] * width
    return call(
        down_kernel, "down", outs, flops, 4 << 20, gate, gate_other, up, up_other, weight
    )


def add_kernel(count, own_ref, *refs):
    total = own_ref[...]
    for ref in refs[:count]:
        total = total + ref[...].astype(F32)
    refs[-1][...] = total.astype(refs[-1].dtype)


def add(own, arrived, dtype, hint=1000000, after=()):
    count = len(arrived)
    return pl.pallas_call(
        functools.partial(add_kernel, count),
        in_specs=[pl.BlockSpec(memory_space=pltpu.VMEM)] * (1 + count)
        + [pl.BlockSpec(memory_space=pl.ANY)] * len(after),
        out_shape=jax.ShapeDtypeStruct(own.shape, dtype),
        compiler_params=pltpu.CompilerParams(vmem_limit_bytes=2 << 20),
        cost_estimate=pl.CostEstimate(flops=hint, bytes_accessed=0, transcendentals=0),
        name="add",
    )(own, *arrived, *after)


def make_local(wide, narrow):
    fars = list(range(4, wide, 4))

    def swap(value, bits):
        return lax.ppermute(value, "wide", [(i, i ^ bits) for i in range(wide)])

    def across_cores(value):
        return lax.ppermute(value, "narrow", [(i, (i + 1) % narrow) for i in range(narrow)])

    def local(tokens, gate_weight, up_weight, down_weight):
        rows = tokens.shape[0]
        block = {0: tokens}
        for far in fars:
            block[far] = swap(tokens, far)
        for near in (1, 2, 3):
            block[near] = swap(tokens, near)
        gate_held, up_held = fetch([gate_weight, up_weight])
        *crossed, gate_held, up_held = lax.optimization_barrier(
            [block[far] for far in fars] + [gate_held, up_held]
        )
        block.update(zip(fars, crossed))
        for far in fars:
            for near in (2, 3, 1):
                block[far + near] = swap(block[far], near)
        stay = [0, 1] + fars
        order = [0, 3, 1, 2] + [far + near for far in fars for near in (0, 2, 1, 3)]
        blocks = [block[b] for b in order]
        gate_part = project(blocks, gate_held)
        up_part = project(blocks, up_held)
        outs = down(
            gate_part, across_cores(gate_part), up_part, across_cores(up_part),
            down_weight, rows, [F32 if b in stay else BF16 for b in order],
        )
        part = dict(zip(order, outs))
        sums = []
        for far in fars:
            quad = [swap(part[far + near], near) for near in (3, 1, 2)]
            sums.append(add(part[far], quad, BF16))
        arrived = [swap(value, far) for value, far in zip(sums, fars)]
        pair = add(part[1], [swap(part[3], 2)], BF16, after=sums)
        total = add(part[0], [swap(part[2], 2)], F32, 1500000000, after=[pair])
        return add(total, [swap(pair, 1)] + arrived, BF16)

    return local


def solution(mesh):
    return jax.shard_map(
        make_local(mesh.shape["wide"], mesh.shape["narrow"]),
        mesh=mesh,
        in_specs=(
            P(("groups", "wide"), "narrow"),
            P("narrow", "wide"),
            P("narrow", "wide"),
            P("wide", "narrow"),
        ),
        out_specs=P(("groups", "wide"), "narrow"),
        check_vma=False,
    )
```

```python
import functools

import jax
import jax.numpy as jnp
from jax import lax
from jax.experimental import pallas as pl
from jax.experimental.pallas import tpu as pltpu
from jax.sharding import PartitionSpec as P

F32 = jnp.float32
BF16 = jnp.bfloat16
HALVES = 2


def call(kernel, name, out_shape, flops, vmem, *operands):
    return pl.pallas_call(
        kernel,
        out_shape=out_shape,
        compiler_params=pltpu.CompilerParams(vmem_limit_bytes=vmem),
        cost_estimate=pl.CostEstimate(flops=flops, bytes_accessed=0, transcendentals=0),
        name=name,
    )(*operands)


def fetch_kernel(pieces, count, *refs):
    sems = refs[-1]
    copies = []
    for n in range(count):
        source, target = refs[n], refs[count + n]
        step = source.shape[0] // pieces
        for i in range(pieces):
            part = pl.ds(i * step, step)
            copies.append(pltpu.make_async_copy(source.at[part], target.at[part], sems.at[n, i]))
    for copy in copies:
        copy.start()
    for copy in copies:
        copy.wait()


def fetch(weights, pieces=4):
    count = len(weights)
    return pl.pallas_call(
        functools.partial(fetch_kernel, pieces, count),
        in_specs=[pl.BlockSpec(memory_space=pl.ANY)] * count,
        out_specs=[pl.BlockSpec(memory_space=pltpu.VMEM)] * count,
        out_shape=[jax.ShapeDtypeStruct(w.shape, w.dtype) for w in weights],
        scratch_shapes=[pltpu.SemaphoreType.DMA((count, pieces))],
        compiler_params=pltpu.CompilerParams(vmem_limit_bytes=43 << 20),
        cost_estimate=pl.CostEstimate(flops=4000000000, bytes_accessed=0, transcendentals=0),
        name="fetch",
    )(*weights)


def project_kernel(*refs):
    *block_refs, weight_ref, out_ref = refs
    rows = jnp.concatenate([ref[...] for ref in block_refs], axis=0)
    out_ref[...] = jnp.dot(rows, weight_ref[...], preferred_element_type=F32)


def project(blocks, weight):
    rows = sum(block.shape[0] for block in blocks)
    out = jax.ShapeDtypeStruct((rows, weight.shape[1]), F32)
    return call(project_kernel, "project", out, 400000000, 4 << 20, *blocks, weight)


def down_kernel(pieces, gate_ref, gate_other_ref, up_ref, up_other_ref, weight_ref, *out_refs):
    gate_sum = gate_ref[...] + gate_other_ref[...]
    up_sum = up_ref[...] + up_other_ref[...]
    hidden = (jax.nn.silu(gate_sum) * up_sum).astype(BF16)
    width = weight_ref.shape[1]
    tile = min(512, width // HALVES)
    rows = out_refs[0].shape[0]
    for first in range(0, width, tile):
        partial = jnp.dot(hidden, weight_ref[:, first:first + tile], preferred_element_type=F32)
        for (row_block, start, size), out_ref in zip(pieces, out_refs):
            if start <= first < start + size:
                piece = partial[row_block * rows:(row_block + 1) * rows]
                out_ref[:, first - start:first - start + tile] = piece.astype(out_ref.dtype)


def down(gate, gate_other, up, up_other, weight, rows, wanted):
    outs = [jax.ShapeDtypeStruct((rows, size), dtype) for _, _, size, dtype in wanted]
    pieces = [piece[:3] for piece in wanted]
    hint = 2 * gate.shape[0] * weight.shape[0] * weight.shape[1]
    return call(
        functools.partial(down_kernel, pieces), "down", outs, hint, 4 << 20,
        gate, gate_other, up, up_other, weight,
    )


def add_kernel(count, own_ref, *refs):
    total = own_ref[...]
    for ref in refs[:count]:
        total = total + ref[...].astype(F32)
    refs[-1][...] = total.astype(refs[-1].dtype)


def add(own, arrived, dtype, hint=1000000, after=()):
    count = len(arrived)
    return pl.pallas_call(
        functools.partial(add_kernel, count),
        in_specs=[pl.BlockSpec(memory_space=pltpu.VMEM)] * (1 + count)
        + [pl.BlockSpec(memory_space=pl.ANY)] * len(after),
        out_shape=jax.ShapeDtypeStruct(own.shape, dtype),
        compiler_params=pltpu.CompilerParams(vmem_limit_bytes=2 << 20),
        cost_estimate=pl.CostEstimate(flops=hint, bytes_accessed=0, transcendentals=0),
        name="add",
    )(own, *arrived, *after)


def early_kernel(near_ref, *refs):
    *far_refs, out_ref = refs
    total = near_ref[:, :out_ref.shape[1]]
    for ref in far_refs:
        total = total + ref[...].astype(F32)
    out_ref[...] = total


def join_kernel(early_ref, near_ref, pair_ref, *refs):
    *far_refs, out_ref = refs
    size = early_ref.shape[1]
    out_ref[:, :size] = (early_ref[...] + pair_ref[:, :size].astype(F32)).astype(out_ref.dtype)
    total = near_ref[:, size:] + pair_ref[:, size:].astype(F32)
    for ref in far_refs:
        total = total + ref[...].astype(F32)
    out_ref[:, size:] = total.astype(out_ref.dtype)


def join(near, pair, first_halves, second_halves):
    rows, width = near.shape
    early = jax.ShapeDtypeStruct((rows, width // HALVES), F32)
    early = call(early_kernel, "early", early, 3000000000, 2 << 20, near, *first_halves)
    out = jax.ShapeDtypeStruct(near.shape, BF16)
    return call(join_kernel, "join", out, 1000000, 2 << 20, early, near, pair, *second_halves)


def make_local(wide, narrow):
    fars = list(range(4, wide, 4))

    def swap(value, bits):
        return lax.ppermute(value, "wide", [(i, i ^ bits) for i in range(wide)])

    def across_cores(value):
        return lax.ppermute(value, "narrow", [(i, (i + 1) % narrow) for i in range(narrow)])

    def local(tokens, gate_weight, up_weight, down_weight):
        rows = tokens.shape[0]
        block = {0: tokens}
        for far in fars:
            block[far] = swap(tokens, far)
        for near in (1, 2, 3):
            block[near] = swap(tokens, near)
        gate_held, up_held = fetch([gate_weight, up_weight])
        *crossed, gate_held, up_held = lax.optimization_barrier(
            [block[far] for far in fars] + [gate_held, up_held]
        )
        block.update(zip(fars, crossed))
        for far in fars:
            for near in (2, 3, 1):
                block[far + near] = swap(block[far], near)
        stay = [0, 1] + fars
        order = [0, 3, 1, 2] + [far + near for far in fars for near in (0, 2, 1, 3)]
        blocks = [block[b] for b in order]
        gate_part = project(blocks, gate_held)
        up_part = project(blocks, up_held)
        width = down_weight.shape[1]
        size = width // HALVES
        names, wanted = [], []
        for at, b in enumerate(order):
            dtype = F32 if b in stay else BF16
            if b < 4:
                names.append((b, 0))
                wanted.append((at, 0, width, dtype))
                continue
            for half in range(HALVES):
                names.append((b, half))
                wanted.append((at, half * size, size, dtype))
        outs = down(
            gate_part, across_cores(gate_part), up_part, across_cores(up_part),
            down_weight, rows, wanted,
        )
        part = dict(zip(names, outs))
        sums = []
        for far in fars:
            for half in range(HALVES):
                quad = [swap(part[far + near, half], near) for near in (3, 1, 2)]
                sums.append(add(part[far, half], quad, BF16, 3000000000))
        part[2, 0], sums[0] = lax.optimization_barrier((part[2, 0], sums[0]))
        arrived = [swap(value, far) for value, far in zip(sums, [f for f in fars for _ in range(HALVES)])]
        pair = add(part[1, 0], [swap(part[3, 0], 2)], BF16, after=sums[:1])
        total = add(part[0, 0], [swap(part[2, 0], 2)], F32, 1500000000, after=sums)
        return join(total, swap(pair, 1), arrived[::2], arrived[1::2])

    return local


def solution(mesh):
    return jax.shard_map(
        make_local(mesh.shape["wide"], mesh.shape["narrow"]),
        mesh=mesh,
        in_specs=(
            P(("groups", "wide"), "narrow"),
            P("narrow", "wide"),
            P("narrow", "wide"),
            P("wide", "narrow"),
        ),
        out_specs=P(("groups", "wide"), "narrow"),
        check_vma=False,
    )
```

```python
import functools

import jax
import jax.numpy as jnp
from jax import lax
from jax.experimental import pallas as pl
from jax.experimental.pallas import tpu as pltpu
from jax.sharding import PartitionSpec as P

F32 = jnp.float32
BF16 = jnp.bfloat16


def call(kernel, name, out_shape, flops, vmem, *operands):
    return pl.pallas_call(
        kernel,
        out_shape=out_shape,
        compiler_params=pltpu.CompilerParams(vmem_limit_bytes=vmem),
        cost_estimate=pl.CostEstimate(flops=flops, bytes_accessed=0, transcendentals=0),
        name=name,
    )(*operands)


def fetch_kernel(pieces, source, target, sems):
    step = source.shape[0] // pieces
    copies = []
    for i in range(pieces):
        part = pl.ds(i * step, step)
        copies.append(pltpu.make_async_copy(source.at[part], target.at[part], sems.at[i]))
    for copy in copies:
        copy.start()
    for copy in copies:
        copy.wait()


def fetch(weight, grant, hint, pieces=8):
    return pl.pallas_call(
        functools.partial(fetch_kernel, pieces),
        in_specs=[pl.BlockSpec(memory_space=pl.ANY)],
        out_specs=pl.BlockSpec(memory_space=pltpu.VMEM),
        out_shape=jax.ShapeDtypeStruct(weight.shape, weight.dtype),
        scratch_shapes=[pltpu.SemaphoreType.DMA((pieces,))],
        compiler_params=pltpu.CompilerParams(vmem_limit_bytes=grant << 20),
        cost_estimate=pl.CostEstimate(flops=hint, bytes_accessed=0, transcendentals=0),
        name="fetch",
    )(weight)


def project_kernel(*refs):
    *block_refs, weight_ref, out_ref = refs
    rows = jnp.concatenate([ref[...] for ref in block_refs], axis=0)
    out_ref[...] = jnp.dot(rows, weight_ref[...], preferred_element_type=F32)


def project(blocks, weight):
    rows = sum(block.shape[0] for block in blocks)
    out = jax.ShapeDtypeStruct((rows, weight.shape[1]), F32)
    return call(project_kernel, "project", out, 400000000, 4 << 20, *blocks, weight)


def down_kernel(gate_ref, gate_other_ref, up_ref, up_other_ref, weight_ref, *out_refs):
    gate_sum = gate_ref[...] + gate_other_ref[...]
    up_sum = up_ref[...] + up_other_ref[...]
    hidden = (jax.nn.silu(gate_sum) * up_sum).astype(BF16)
    width = weight_ref.shape[1]
    tile = min(512, width)
    rows = out_refs[0].shape[0]

    def column_tile(step, carry):
        columns = pl.ds(pl.multiple_of(step * tile, tile), tile)
        partial = jnp.dot(hidden, weight_ref[:, columns], preferred_element_type=F32)
        for k, out_ref in enumerate(out_refs):
            out_ref[:, columns] = partial[k * rows:(k + 1) * rows].astype(out_ref.dtype)
        return carry

    lax.fori_loop(0, width // tile, column_tile, 0, unroll=True)


def down(gate, gate_other, up, up_other, weight, rows, dtypes):
    width = weight.shape[1]
    outs = [jax.ShapeDtypeStruct((rows, width), dtype) for dtype in dtypes]
    flops = 2 * gate.shape[0] * weight.shape[0] * width
    return call(
        down_kernel, "down", outs, flops, 4 << 20, gate, gate_other, up, up_other, weight
    )


def add_kernel(count, own_ref, *refs):
    total = own_ref[...]
    for ref in refs[:count]:
        total = total + ref[...].astype(F32)
    refs[-1][...] = total.astype(refs[-1].dtype)


def add(own, arrived, dtype, hint=1000000, after=()):
    count = len(arrived)
    return pl.pallas_call(
        functools.partial(add_kernel, count),
        in_specs=[pl.BlockSpec(memory_space=pltpu.VMEM)] * (1 + count)
        + [pl.BlockSpec(memory_space=pl.ANY)] * len(after),
        out_shape=jax.ShapeDtypeStruct(own.shape, dtype),
        compiler_params=pltpu.CompilerParams(vmem_limit_bytes=2 << 20),
        cost_estimate=pl.CostEstimate(flops=hint, bytes_accessed=0, transcendentals=0),
        name="add",
    )(own, *arrived, *after)


def make_local(wide, narrow):
    fars = list(range(4, wide, 4))

    def swap(value, bits):
        return lax.ppermute(value, "wide", [(i, i ^ bits) for i in range(wide)])

    def across_cores(value):
        return lax.ppermute(value, "narrow", [(i, (i + 1) % narrow) for i in range(narrow)])

    def local(tokens, gate_weight, up_weight, down_weight):
        rows = tokens.shape[0]
        block = {0: tokens}
        for far in fars:
            block[far] = swap(tokens, far)
        for near in (1, 2, 3):
            block[near] = swap(tokens, near)
        gate_held = fetch(gate_weight, 48, 2000000000)
        up_held = fetch(up_weight, 48, 2000000000)
        *crossed, gate_held = lax.optimization_barrier([block[far] for far in fars] + [gate_held])
        block.update(zip(fars, crossed))
        for far in fars:
            for near in (2, 3, 1):
                block[far + near] = swap(block[far], near)
        stay = [0, 1] + fars
        order = [0, 3, 1, 2] + [far + near for far in fars for near in (0, 2, 1, 3)]
        blocks = [block[b] for b in order]
        gate_part = project(blocks, gate_held)
        up_part = project(blocks, up_held)
        outs = down(
            gate_part, across_cores(gate_part), up_part, across_cores(up_part),
            down_weight, rows, [F32 if b in stay else BF16 for b in order],
        )
        part = dict(zip(order, outs))
        sums = []
        for far in fars:
            quad = [swap(part[far + near], near) for near in (3, 1, 2)]
            sums.append(add(part[far], quad, BF16))
        arrived = [swap(value, far) for value, far in zip(sums, fars)]
        pair = add(part[1], [swap(part[3], 2)], BF16, after=sums)
        total = add(part[0], [swap(part[2], 2)], F32, 1500000000, after=[pair])
        return add(total, [swap(pair, 1)] + arrived, BF16)

    return local


def solution(mesh):
    return jax.shard_map(
        make_local(mesh.shape["wide"], mesh.shape["narrow"]),
        mesh=mesh,
        in_specs=(
            P(("groups", "wide"), "narrow"),
            P("narrow", "wide"),
            P("narrow", "wide"),
            P("wide", "narrow"),
        ),
        out_specs=P(("groups", "wide"), "narrow"),
        check_vma=False,
    )
```

```python
import functools

import jax
import jax.numpy as jnp
from jax import lax
from jax.experimental import pallas as pl
from jax.experimental.pallas import tpu as pltpu
from jax.sharding import PartitionSpec as P

F32 = jnp.float32
BF16 = jnp.bfloat16


def call(kernel, name, out_shape, flops, vmem, *operands):
    return pl.pallas_call(
        kernel,
        out_shape=out_shape,
        compiler_params=pltpu.CompilerParams(vmem_limit_bytes=vmem),
        cost_estimate=pl.CostEstimate(flops=flops, bytes_accessed=0, transcendentals=0),
        name=name,
    )(*operands)


def fetch_kernel(pieces, source, target, sems):
    step = source.shape[0] // pieces
    copies = []
    for i in range(pieces):
        part = pl.ds(i * step, step)
        copies.append(pltpu.make_async_copy(source.at[part], target.at[part], sems.at[i]))
    for copy in copies:
        copy.start()
    for copy in copies:
        copy.wait()


def fetch(weight, grant, hint, pieces=8):
    return pl.pallas_call(
        functools.partial(fetch_kernel, pieces),
        in_specs=[pl.BlockSpec(memory_space=pl.ANY)],
        out_specs=pl.BlockSpec(memory_space=pltpu.VMEM),
        out_shape=jax.ShapeDtypeStruct(weight.shape, weight.dtype),
        scratch_shapes=[pltpu.SemaphoreType.DMA((pieces,))],
        compiler_params=pltpu.CompilerParams(vmem_limit_bytes=grant << 20),
        cost_estimate=pl.CostEstimate(flops=hint, bytes_accessed=0, transcendentals=0),
        name="fetch",
    )(weight)


def project_kernel(*refs):
    *block_refs, weight_ref, out_ref = refs
    rows = jnp.concatenate([ref[...] for ref in block_refs], axis=0)
    out_ref[...] = jnp.dot(rows, weight_ref[...], preferred_element_type=F32)


def project(blocks, weight):
    rows = sum(block.shape[0] for block in blocks)
    out = jax.ShapeDtypeStruct((rows, weight.shape[1]), F32)
    return call(project_kernel, "project", out, 400000000, 4 << 20, *blocks, weight)


def down_kernel(gate_ref, gate_other_ref, up_ref, up_other_ref, weight_ref, *out_refs):
    gate_sum = gate_ref[...] + gate_other_ref[...]
    up_sum = up_ref[...] + up_other_ref[...]
    hidden = (jax.nn.silu(gate_sum) * up_sum).astype(BF16)
    width = weight_ref.shape[1]
    tile = min(512, width)
    rows = out_refs[0].shape[0]

    def column_tile(step, carry):
        columns = pl.ds(pl.multiple_of(step * tile, tile), tile)
        partial = jnp.dot(hidden, weight_ref[:, columns], preferred_element_type=F32)
        for k, out_ref in enumerate(out_refs):
            out_ref[:, columns] = partial[k * rows:(k + 1) * rows].astype(out_ref.dtype)
        return carry

    lax.fori_loop(0, width // tile, column_tile, 0, unroll=True)


def down(gate, gate_other, up, up_other, weight, rows, dtypes):
    width = weight.shape[1]
    outs = [jax.ShapeDtypeStruct((rows, width), dtype) for dtype in dtypes]
    flops = 2 * gate.shape[0] * weight.shape[0] * width
    return call(
        down_kernel, "down", outs, flops, 4 << 20, gate, gate_other, up, up_other, weight
    )


def add_kernel(count, own_ref, *refs):
    total = own_ref[...]
    for ref in refs[:count]:
        total = total + ref[...].astype(F32)
    refs[-1][...] = total.astype(refs[-1].dtype)


def add(own, arrived, dtype, hint=1000000, after=()):
    count = len(arrived)
    return pl.pallas_call(
        functools.partial(add_kernel, count),
        in_specs=[pl.BlockSpec(memory_space=pltpu.VMEM)] * (1 + count)
        + [pl.BlockSpec(memory_space=pl.ANY)] * len(after),
        out_shape=jax.ShapeDtypeStruct(own.shape, dtype),
        compiler_params=pltpu.CompilerParams(vmem_limit_bytes=2 << 20),
        cost_estimate=pl.CostEstimate(flops=hint, bytes_accessed=0, transcendentals=0),
        name="add",
    )(own, *arrived, *after)


def add_in_turn_kernel(count, core_ref, own_ref, other_ref, *refs):
    first_ref, second_ref = refs[-2:]
    total = own_ref[...]
    for ref in refs[:count]:
        total = total + ref[...].astype(F32)
    total = total.astype(first_ref.dtype)

    @pl.when(core_ref[0] == 0)
    def _():
        first_ref[...] = total
        second_ref[...] = other_ref[...]

    @pl.when(core_ref[0] != 0)
    def _():
        first_ref[...] = other_ref[...]
        second_ref[...] = total


def add_in_turn(core, own, arrived, other):
    out = jax.ShapeDtypeStruct(own.shape, BF16)
    return pl.pallas_call(
        functools.partial(add_in_turn_kernel, len(arrived)),
        in_specs=[pl.BlockSpec(memory_space=pltpu.SMEM)]
        + [pl.BlockSpec(memory_space=pltpu.VMEM)] * (2 + len(arrived)),
        out_shape=[out, out],
        compiler_params=pltpu.CompilerParams(vmem_limit_bytes=2 << 20),
        cost_estimate=pl.CostEstimate(flops=1000000, bytes_accessed=0, transcendentals=0),
        name="add_in_turn",
    )(core, own, other, *arrived)


def make_local(wide, narrow):
    fars = list(range(4, wide, 4))

    def swap(value, bits):
        return lax.ppermute(value, "wide", [(i, i ^ bits) for i in range(wide)])

    def swap_by_core(value, bits, other_bits):
        pairs = []
        for i in range(wide):
            for core in range(narrow):
                target = i ^ (other_bits if core else bits)
                pairs.append((i * narrow + core, target * narrow + core))
        return lax.ppermute(value, ("wide", "narrow"), pairs)

    def across_cores(value):
        return lax.ppermute(value, "narrow", [(i, (i + 1) % narrow) for i in range(narrow)])

    def local(tokens, gate_weight, up_weight, down_weight):
        rows = tokens.shape[0]
        block = {0: tokens}
        for far in fars:
            block[far] = swap(tokens, far)
        for near in (1, 2, 3):
            block[near] = swap(tokens, near)
        gate_held = fetch(gate_weight, 48, 2000000000)
        up_held = fetch(up_weight, 48, 2000000000)
        *crossed, gate_held = lax.optimization_barrier([block[far] for far in fars] + [gate_held])
        block.update(zip(fars, crossed))
        for far in fars:
            for near in (2, 3, 1):
                block[far + near] = swap(block[far], near)
        stay = [0, 1] + fars
        order = [0, 3, 1, 2] + [far + near for far in fars for near in (0, 2, 1, 3)]
        blocks = [block[b] for b in order]
        gate_part = project(blocks, gate_held)
        up_part = project(blocks, up_held)
        outs = down(
            gate_part, across_cores(gate_part), up_part, across_cores(up_part),
            down_weight, rows, [F32 if b in stay else BF16 for b in order],
        )
        part = dict(zip(order, outs))
        core = lax.axis_index("narrow").reshape(1)
        sums, arrived = [], []
        for far in fars:
            quad = [swap(part[far + near], near) for near in (2, 3, 1)]
            if sums:
                sums.append(add(part[far], quad, BF16))
                arrived.append(swap(sums[-1], far))
                continue
            sums = list(add_in_turn(core, part[far], quad, part[2]))
            arrived = [swap_by_core(sums[0], far, 2), swap_by_core(sums[1], 2, far)]
        pair = add(part[1], [swap(part[3], 2)], BF16, after=sums)
        total = add(part[0], arrived, F32, 3000000000)
        return add(total, [swap(pair, 1)], BF16)

    return local


def solution(mesh):
    return jax.shard_map(
        make_local(mesh.shape["wide"], mesh.shape["narrow"]),
        mesh=mesh,
        in_specs=(
            P(("groups", "wide"), "narrow"),
            P("narrow", "wide"),
            P("narrow", "wide"),
            P("wide", "narrow"),
        ),
        out_specs=P(("groups", "wide"), "narrow"),
        check_vma=False,
    )
```

```python
import functools

import jax
import jax.numpy as jnp
from jax import lax
from jax.experimental import pallas as pl
from jax.experimental.pallas import tpu as pltpu
from jax.sharding import PartitionSpec as P

F32 = jnp.float32
BF16 = jnp.bfloat16


def call(kernel, name, out_shape, flops, vmem, *operands):
    return pl.pallas_call(
        kernel,
        out_shape=out_shape,
        compiler_params=pltpu.CompilerParams(vmem_limit_bytes=vmem),
        cost_estimate=pl.CostEstimate(flops=flops, bytes_accessed=0, transcendentals=0),
        name=name,
    )(*operands)


def fetch_kernel(pieces, source, target, sems):
    step = source.shape[0] // pieces
    copies = []
    for i in range(pieces):
        part = pl.ds(i * step, step)
        copies.append(pltpu.make_async_copy(source.at[part], target.at[part], sems.at[i]))
    for copy in copies:
        copy.start()
    for copy in copies:
        copy.wait()


def fetch(weight, grant, hint, pieces=8):
    return pl.pallas_call(
        functools.partial(fetch_kernel, pieces),
        in_specs=[pl.BlockSpec(memory_space=pl.ANY)],
        out_specs=pl.BlockSpec(memory_space=pltpu.VMEM),
        out_shape=jax.ShapeDtypeStruct(weight.shape, weight.dtype),
        scratch_shapes=[pltpu.SemaphoreType.DMA((pieces,))],
        compiler_params=pltpu.CompilerParams(vmem_limit_bytes=grant << 20),
        cost_estimate=pl.CostEstimate(flops=hint, bytes_accessed=0, transcendentals=0),
        name="fetch",
    )(weight)


def project_kernel(*refs):
    *block_refs, weight_ref, out_ref = refs
    rows = jnp.concatenate([ref[...] for ref in block_refs], axis=0)
    out_ref[...] = jnp.dot(rows, weight_ref[...], preferred_element_type=F32)


def project(blocks, weight):
    rows = sum(block.shape[0] for block in blocks)
    out = jax.ShapeDtypeStruct((rows, weight.shape[1]), F32)
    return call(project_kernel, "project", out, 400000000, 4 << 20, *blocks, weight)


def down_kernel(gate_ref, gate_other_ref, up_ref, up_other_ref, weight_ref, *out_refs):
    gate_sum = gate_ref[...] + gate_other_ref[...]
    up_sum = up_ref[...] + up_other_ref[...]
    hidden = (jax.nn.silu(gate_sum) * up_sum).astype(BF16)
    width = weight_ref.shape[1]
    tile = min(512, width)
    rows = out_refs[0].shape[0]

    def column_tile(step, carry):
        columns = pl.ds(pl.multiple_of(step * tile, tile), tile)
        partial = jnp.dot(hidden, weight_ref[:, columns], preferred_element_type=F32)
        for k, out_ref in enumerate(out_refs):
            out_ref[:, columns] = partial[k * rows:(k + 1) * rows].astype(out_ref.dtype)
        return carry

    lax.fori_loop(0, width // tile, column_tile, 0, unroll=True)


def down(gate, gate_other, up, up_other, weight, rows, dtypes):
    width = weight.shape[1]
    outs = [jax.ShapeDtypeStruct((rows, width), dtype) for dtype in dtypes]
    flops = 2 * gate.shape[0] * weight.shape[0] * width
    return call(
        down_kernel, "down", outs, flops, 4 << 20, gate, gate_other, up, up_other, weight
    )


def add_kernel(count, own_ref, *refs):
    total = own_ref[...]
    for ref in refs[:count]:
        total = total + ref[...].astype(F32)
    refs[-1][...] = total.astype(refs[-1].dtype)


def add(own, arrived, dtype, hint=1000000, after=()):
    count = len(arrived)
    return pl.pallas_call(
        functools.partial(add_kernel, count),
        in_specs=[pl.BlockSpec(memory_space=pltpu.VMEM)] * (1 + count)
        + [pl.BlockSpec(memory_space=pl.ANY)] * len(after),
        out_shape=jax.ShapeDtypeStruct(own.shape, dtype),
        compiler_params=pltpu.CompilerParams(vmem_limit_bytes=2 << 20),
        cost_estimate=pl.CostEstimate(flops=hint, bytes_accessed=0, transcendentals=0),
        name="add",
    )(own, *arrived, *after)


def make_local(wide, narrow):
    fars = list(range(4, wide, 4))

    def swap(value, bits):
        return lax.ppermute(value, "wide", [(i, i ^ bits) for i in range(wide)])

    def across_cores(value):
        return lax.ppermute(value, "narrow", [(i, (i + 1) % narrow) for i in range(narrow)])

    def local(tokens, gate_weight, up_weight, down_weight):
        rows = tokens.shape[0]
        block = {0: tokens}
        for far in fars:
            block[far] = swap(tokens, far)
        for near in (1, 2):
            block[near] = swap(tokens, near)
        gate_held = fetch(gate_weight, 48, 2000000000)
        up_held = fetch(up_weight, 48, 2000000000)
        own, gate_held = lax.optimization_barrier((tokens, gate_held))
        block[3] = swap(own, 3)
        *crossed, gate_held = lax.optimization_barrier([block[far] for far in fars] + [gate_held])
        block.update(zip(fars, crossed))
        for far in fars:
            for near in (2, 3, 1):
                block[far + near] = swap(block[far], near)
        stay = [0, 1] + fars
        order = [0, 3, 1, 2] + [far + near for far in fars for near in (0, 2, 1, 3)]
        blocks = [block[b] for b in order]
        gate_part = project(blocks, gate_held)
        up_part = project(blocks, up_held)
        outs = down(
            gate_part, across_cores(gate_part), up_part, across_cores(up_part),
            down_weight, rows, [F32 if b in stay else BF16 for b in order],
        )
        part = dict(zip(order, outs))
        sums = []
        for far in fars:
            quad = [swap(part[far + near], near) for near in (3, 1, 2)]
            sums.append(add(part[far], quad, BF16))
        arrived = [swap(value, far) for value, far in zip(sums, fars)]
        pair = add(part[1], [swap(part[3], 2)], BF16, after=sums)
        total = add(part[0], [swap(part[2], 2)], F32, 1500000000, after=[pair])
        return add(total, [swap(pair, 1)] + arrived, BF16)

    return local


def solution(mesh):
    return jax.shard_map(
        make_local(mesh.shape["wide"], mesh.shape["narrow"]),
        mesh=mesh,
        in_specs=(
            P(("groups", "wide"), "narrow"),
            P("narrow", "wide"),
            P("narrow", "wide"),
            P("wide", "narrow"),
        ),
        out_specs=P(("groups", "wide"), "narrow"),
        check_vma=False,
    )
```

```python
import functools

import jax
import jax.numpy as jnp
from jax import lax
from jax.experimental import pallas as pl
from jax.experimental.pallas import tpu as pltpu
from jax.sharding import PartitionSpec as P

F32 = jnp.float32
BF16 = jnp.bfloat16


def call(kernel, name, out_shape, flops, vmem, *operands):
    return pl.pallas_call(
        kernel,
        out_shape=out_shape,
        compiler_params=pltpu.CompilerParams(vmem_limit_bytes=vmem),
        cost_estimate=pl.CostEstimate(flops=flops, bytes_accessed=0, transcendentals=0),
        name=name,
    )(*operands)


def fetch_kernel(pieces, source, target, sems):
    step = source.shape[0] // pieces
    copies = []
    for i in range(pieces):
        part = pl.ds(i * step, step)
        copies.append(pltpu.make_async_copy(source.at[part], target.at[part], sems.at[i]))
    for copy in copies:
        copy.start()
    for copy in copies:
        copy.wait()


def fetch(weight, grant, hint, pieces=8):
    return pl.pallas_call(
        functools.partial(fetch_kernel, pieces),
        in_specs=[pl.BlockSpec(memory_space=pl.ANY)],
        out_specs=pl.BlockSpec(memory_space=pltpu.VMEM),
        out_shape=jax.ShapeDtypeStruct(weight.shape, weight.dtype),
        scratch_shapes=[pltpu.SemaphoreType.DMA((pieces,))],
        compiler_params=pltpu.CompilerParams(vmem_limit_bytes=grant << 20),
        cost_estimate=pl.CostEstimate(flops=hint, bytes_accessed=0, transcendentals=0),
        name="fetch",
    )(weight)


def project_kernel(*refs):
    *block_refs, weight_ref, out_ref = refs
    rows = jnp.concatenate([ref[...] for ref in block_refs], axis=0)
    out_ref[...] = jnp.dot(rows, weight_ref[...], preferred_element_type=F32)


def project(blocks, weight):
    rows = sum(block.shape[0] for block in blocks)
    out = jax.ShapeDtypeStruct((rows, weight.shape[1]), F32)
    return call(project_kernel, "project", out, 400000000, 4 << 20, *blocks, weight)


def down_kernel(gate_ref, gate_other_ref, up_ref, up_other_ref, weight_ref, *out_refs):
    gate_sum = gate_ref[...] + gate_other_ref[...]
    up_sum = up_ref[...] + up_other_ref[...]
    hidden = (jax.nn.silu(gate_sum) * up_sum).astype(BF16)
    width = weight_ref.shape[1]
    tile = min(512, width)
    rows = out_refs[0].shape[0]

    def column_tile(step, carry):
        columns = pl.ds(pl.multiple_of(step * tile, tile), tile)
        partial = jnp.dot(hidden, weight_ref[:, columns], preferred_element_type=F32)
        for k, out_ref in enumerate(out_refs):
            out_ref[:, columns] = partial[k * rows:(k + 1) * rows].astype(out_ref.dtype)
        return carry

    lax.fori_loop(0, width // tile, column_tile, 0, unroll=True)


def down(gate, gate_other, up, up_other, weight, rows, dtypes):
    width = weight.shape[1]
    outs = [jax.ShapeDtypeStruct((rows, width), dtype) for dtype in dtypes]
    flops = 2 * gate.shape[0] * weight.shape[0] * width
    return call(
        down_kernel, "down", outs, flops, 4 << 20, gate, gate_other, up, up_other, weight
    )


def add_kernel(count, own_ref, *refs):
    total = own_ref[...]
    for ref in refs[:count]:
        total = total + ref[...].astype(F32)
    refs[-1][...] = total.astype(refs[-1].dtype)


def add(own, arrived, dtype, hint=1000000, after=()):
    count = len(arrived)
    return pl.pallas_call(
        functools.partial(add_kernel, count),
        in_specs=[pl.BlockSpec(memory_space=pltpu.VMEM)] * (1 + count)
        + [pl.BlockSpec(memory_space=pl.ANY)] * len(after),
        out_shape=jax.ShapeDtypeStruct(own.shape, dtype),
        compiler_params=pltpu.CompilerParams(vmem_limit_bytes=2 << 20),
        cost_estimate=pl.CostEstimate(flops=hint, bytes_accessed=0, transcendentals=0),
        name="add",
    )(own, *arrived, *after)


def make_local(wide, narrow):
    fars = list(range(4, wide, 4))

    def swap(value, bits):
        return lax.ppermute(value, "wide", [(i, i ^ bits) for i in range(wide)])

    def across_cores(value):
        return lax.ppermute(value, "narrow", [(i, (i + 1) % narrow) for i in range(narrow)])

    def local(tokens, gate_weight, up_weight, down_weight):
        rows = tokens.shape[0]
        block = {0: tokens}
        for far in fars:
            block[far] = swap(tokens, far)
        for near in (1, 2):
            block[near] = swap(tokens, near)
        gate_held = fetch(gate_weight, 48, 2000000000)
        up_held = fetch(up_weight, 48, 2000000000)
        own, gate_held = lax.optimization_barrier((tokens, gate_held))
        block[3] = swap(own, 3)
        *crossed, gate_held = lax.optimization_barrier([block[far] for far in fars] + [gate_held])
        block.update(zip(fars, crossed))
        for far in fars:
            for near in (2, 3, 1):
                block[far + near] = swap(block[far], near)
        stay = [0, 1] + fars
        order = [0, 3, 1, 2] + [far + near for far in fars for near in (0, 2, 1, 3)]
        blocks = [block[b] for b in order]
        gate_part = project(blocks, gate_held)
        up_part = project(blocks, up_held)
        outs = down(
            gate_part, across_cores(gate_part), up_part, across_cores(up_part),
            down_weight, rows, [F32 if b in stay else BF16 for b in order],
        )
        part = dict(zip(order, outs))
        sums, direct = [], []
        for far in fars:
            sums.append(add(part[far], [swap(part[far + near], near) for near in (1, 2)], BF16))
            direct.append(swap(part[far + 3], far + 3))
        arrived = [swap(value, far) for value, far in zip(sums, fars)]
        pair = add(part[1], [swap(part[3], 2)], BF16, after=sums)
        total = add(part[0], direct + [swap(part[2], 2)], F32, 1500000000, after=[pair])
        return add(total, [swap(pair, 1)] + arrived, BF16)

    return local


def solution(mesh):
    return jax.shard_map(
        make_local(mesh.shape["wide"], mesh.shape["narrow"]),
        mesh=mesh,
        in_specs=(
            P(("groups", "wide"), "narrow"),
            P("narrow", "wide"),
            P("narrow", "wide"),
            P("wide", "narrow"),
        ),
        out_specs=P(("groups", "wide"), "narrow"),
        check_vma=False,
    )
```

```python
import functools

import jax
import jax.numpy as jnp
from jax import lax
from jax.experimental import pallas as pl
from jax.experimental.pallas import tpu as pltpu
from jax.sharding import PartitionSpec as P

F32 = jnp.float32
BF16 = jnp.bfloat16


def call(kernel, name, out_shape, flops, vmem, *operands):
    return pl.pallas_call(
        kernel,
        out_shape=out_shape,
        compiler_params=pltpu.CompilerParams(vmem_limit_bytes=vmem),
        cost_estimate=pl.CostEstimate(flops=flops, bytes_accessed=0, transcendentals=0),
        name=name,
    )(*operands)


def fetch_kernel(pieces, source, target, sems):
    step = source.shape[0] // pieces
    copies = []
    for i in range(pieces):
        part = pl.ds(i * step, step)
        copies.append(pltpu.make_async_copy(source.at[part], target.at[part], sems.at[i]))
    for copy in copies:
        copy.start()
    for copy in copies:
        copy.wait()


def fetch(weight, grant, hint, pieces=8):
    return pl.pallas_call(
        functools.partial(fetch_kernel, pieces),
        in_specs=[pl.BlockSpec(memory_space=pl.ANY)],
        out_specs=pl.BlockSpec(memory_space=pltpu.VMEM),
        out_shape=jax.ShapeDtypeStruct(weight.shape, weight.dtype),
        scratch_shapes=[pltpu.SemaphoreType.DMA((pieces,))],
        compiler_params=pltpu.CompilerParams(vmem_limit_bytes=grant << 20),
        cost_estimate=pl.CostEstimate(flops=hint, bytes_accessed=0, transcendentals=0),
        name="fetch",
    )(weight)


def project_kernel(*refs):
    *block_refs, weight_ref, out_ref = refs
    rows = jnp.concatenate([ref[...] for ref in block_refs], axis=0)
    out_ref[...] = jnp.dot(rows, weight_ref[...], preferred_element_type=F32)


def project(blocks, weight):
    rows = sum(block.shape[0] for block in blocks)
    out = jax.ShapeDtypeStruct((rows, weight.shape[1]), F32)
    return call(project_kernel, "project", out, 400000000, 4 << 20, *blocks, weight)


def down_kernel(gate_ref, gate_other_ref, up_ref, up_other_ref, weight_ref, *out_refs):
    gate_sum = gate_ref[...] + gate_other_ref[...]
    up_sum = up_ref[...] + up_other_ref[...]
    hidden = (jax.nn.silu(gate_sum) * up_sum).astype(BF16)
    width = weight_ref.shape[1]
    tile = min(512, width)
    rows = out_refs[0].shape[0]

    def column_tile(step, carry):
        columns = pl.ds(pl.multiple_of(step * tile, tile), tile)
        partial = jnp.dot(hidden, weight_ref[:, columns], preferred_element_type=F32)
        for k, out_ref in enumerate(out_refs):
            out_ref[:, columns] = partial[k * rows:(k + 1) * rows].astype(out_ref.dtype)
        return carry

    lax.fori_loop(0, width // tile, column_tile, 0, unroll=True)


def down(gate, gate_other, up, up_other, weight, rows, dtypes):
    width = weight.shape[1]
    outs = [jax.ShapeDtypeStruct((rows, width), dtype) for dtype in dtypes]
    flops = 2 * gate.shape[0] * weight.shape[0] * width
    return call(
        down_kernel, "down", outs, flops, 4 << 20, gate, gate_other, up, up_other, weight
    )


def add_kernel(count, own_ref, *refs):
    total = own_ref[...]
    for ref in refs[:count]:
        total = total + ref[...].astype(F32)
    refs[-1][...] = total.astype(refs[-1].dtype)


def add(own, arrived, dtype, hint=1000000, after=()):
    count = len(arrived)
    return pl.pallas_call(
        functools.partial(add_kernel, count),
        in_specs=[pl.BlockSpec(memory_space=pltpu.VMEM)] * (1 + count)
        + [pl.BlockSpec(memory_space=pl.ANY)] * len(after),
        out_shape=jax.ShapeDtypeStruct(own.shape, dtype),
        compiler_params=pltpu.CompilerParams(vmem_limit_bytes=2 << 20),
        cost_estimate=pl.CostEstimate(flops=hint, bytes_accessed=0, transcendentals=0),
        name="add",
    )(own, *arrived, *after)


def make_local(wide, narrow):
    fars = list(range(4, wide, 4))

    def swap(value, bits):
        return lax.ppermute(value, "wide", [(i, i ^ bits) for i in range(wide)])

    def across_cores(value):
        return lax.ppermute(value, "narrow", [(i, (i + 1) % narrow) for i in range(narrow)])

    def local(tokens, gate_weight, up_weight, down_weight):
        rows = tokens.shape[0]
        block = {0: tokens}
        for far in fars:
            block[far] = swap(tokens, far)
        for near in (1, 2):
            block[near] = swap(tokens, near)
        gate_held = fetch(gate_weight, 48, 2000000000)
        up_held = fetch(up_weight, 48, 2000000000)
        own, gate_held = lax.optimization_barrier((tokens, gate_held))
        block[3] = swap(own, 3)
        *crossed, gate_held = lax.optimization_barrier([block[far] for far in fars] + [gate_held])
        block.update(zip(fars, crossed))
        for far in fars:
            for near in (2, 3, 1):
                block[far + near] = swap(block[far], near)
        stay = [0, 2] + fars
        order = [0, 3, 1, 2] + [far + near for far in fars for near in (0, 2, 1, 3)]
        blocks = [block[b] for b in order]
        gate_part = project(blocks, gate_held)
        up_part = project(blocks, up_held)
        outs = down(
            gate_part, across_cores(gate_part), up_part, across_cores(up_part),
            down_weight, rows, [F32 if b in stay else BF16 for b in order],
        )
        part = dict(zip(order, outs))
        sums, direct = [], []
        for far in fars:
            sums.append(add(part[far], [swap(part[far + near], near) for near in (1, 2)], BF16))
            direct.append(swap(part[far + 3], far + 3))
        arrived = [swap(value, far) for value, far in zip(sums, fars)]
        pair = add(part[2], [swap(part[3], 1)], BF16, after=sums)
        total = add(part[0], direct + [swap(part[1], 1)], F32, 1500000000, after=[pair])
        return add(total, [swap(pair, 2)] + arrived, BF16)

    return local


def solution(mesh):
    return jax.shard_map(
        make_local(mesh.shape["wide"], mesh.shape["narrow"]),
        mesh=mesh,
        in_specs=(
            P(("groups", "wide"), "narrow"),
            P("narrow", "wide"),
            P("narrow", "wide"),
            P("wide", "narrow"),
        ),
        out_specs=P(("groups", "wide"), "narrow"),
        check_vma=False,
    )
```

```python
import functools

import jax
import jax.numpy as jnp
from jax import lax
from jax.experimental import pallas as pl
from jax.experimental.pallas import tpu as pltpu
from jax.sharding import PartitionSpec as P

F32 = jnp.float32
BF16 = jnp.bfloat16


def call(kernel, name, out_shape, flops, vmem, *operands):
    return pl.pallas_call(
        kernel,
        out_shape=out_shape,
        compiler_params=pltpu.CompilerParams(vmem_limit_bytes=vmem),
        cost_estimate=pl.CostEstimate(flops=flops, bytes_accessed=0, transcendentals=0),
        name=name,
    )(*operands)


def fetch_kernel(pieces, source, target, sems):
    step = source.shape[0] // pieces
    copies = []
    for i in range(pieces):
        part = pl.ds(i * step, step)
        copies.append(pltpu.make_async_copy(source.at[part], target.at[part], sems.at[i]))
    for copy in copies:
        copy.start()
    for copy in copies:
        copy.wait()


def fetch(weight, grant, hint, pieces=8):
    return pl.pallas_call(
        functools.partial(fetch_kernel, pieces),
        in_specs=[pl.BlockSpec(memory_space=pl.ANY)],
        out_specs=pl.BlockSpec(memory_space=pltpu.VMEM),
        out_shape=jax.ShapeDtypeStruct(weight.shape, weight.dtype),
        scratch_shapes=[pltpu.SemaphoreType.DMA((pieces,))],
        compiler_params=pltpu.CompilerParams(vmem_limit_bytes=grant << 20),
        cost_estimate=pl.CostEstimate(flops=hint, bytes_accessed=0, transcendentals=0),
        name="fetch",
    )(weight)


def project_kernel(*refs):
    *block_refs, weight_ref, out_ref = refs
    rows = jnp.concatenate([ref[...] for ref in block_refs], axis=0)
    out_ref[...] = jnp.dot(rows, weight_ref[...], preferred_element_type=F32)


def project(blocks, weight):
    rows = sum(block.shape[0] for block in blocks)
    out = jax.ShapeDtypeStruct((rows, weight.shape[1]), F32)
    return call(project_kernel, "project", out, 400000000, 4 << 20, *blocks, weight)


def down_kernel(gate_ref, gate_other_ref, up_ref, up_other_ref, weight_ref, *out_refs):
    gate_sum = gate_ref[...] + gate_other_ref[...]
    up_sum = up_ref[...] + up_other_ref[...]
    hidden = (jax.nn.silu(gate_sum) * up_sum).astype(BF16)
    width = weight_ref.shape[1]
    tile = min(512, width)
    rows = out_refs[0].shape[0]

    def column_tile(step, carry):
        columns = pl.ds(pl.multiple_of(step * tile, tile), tile)
        partial = jnp.dot(hidden, weight_ref[:, columns], preferred_element_type=F32)
        for k, out_ref in enumerate(out_refs):
            out_ref[:, columns] = partial[k * rows:(k + 1) * rows].astype(out_ref.dtype)
        return carry

    lax.fori_loop(0, width // tile, column_tile, 0, unroll=True)


def down(gate, gate_other, up, up_other, weight, rows, dtypes):
    width = weight.shape[1]
    outs = [jax.ShapeDtypeStruct((rows, width), dtype) for dtype in dtypes]
    flops = 2 * gate.shape[0] * weight.shape[0] * width
    return call(
        down_kernel, "down", outs, flops, 4 << 20, gate, gate_other, up, up_other, weight
    )


def add_kernel(count, own_ref, *refs):
    total = own_ref[...]
    for ref in refs[:count]:
        total = total + ref[...].astype(F32)
    refs[-1][...] = total.astype(refs[-1].dtype)


def add(own, arrived, dtype, hint=1000000, after=()):
    count = len(arrived)
    return pl.pallas_call(
        functools.partial(add_kernel, count),
        in_specs=[pl.BlockSpec(memory_space=pltpu.VMEM)] * (1 + count)
        + [pl.BlockSpec(memory_space=pl.ANY)] * len(after),
        out_shape=jax.ShapeDtypeStruct(own.shape, dtype),
        compiler_params=pltpu.CompilerParams(vmem_limit_bytes=2 << 20),
        cost_estimate=pl.CostEstimate(flops=hint, bytes_accessed=0, transcendentals=0),
        name="add",
    )(own, *arrived, *after)


def make_local(wide, narrow):
    fars = list(range(4, wide, 4))

    def swap(value, bits):
        return lax.ppermute(value, "wide", [(i, i ^ bits) for i in range(wide)])

    def across_cores(value):
        return lax.ppermute(value, "narrow", [(i, (i + 1) % narrow) for i in range(narrow)])

    def local(tokens, gate_weight, up_weight, down_weight):
        rows = tokens.shape[0]
        block = {0: tokens}
        for far in fars:
            block[far] = swap(tokens, far)
        for near in (1, 2):
            block[near] = swap(tokens, near)
        gate_held = fetch(gate_weight, 48, 2000000000)
        up_held = fetch(up_weight, 48, 2000000000)
        own, gate_held = lax.optimization_barrier((tokens, gate_held))
        block[3] = swap(own, 3)
        *crossed, gate_held = lax.optimization_barrier([block[far] for far in fars] + [gate_held])
        block.update(zip(fars, crossed))
        for far in fars:
            for near in (2, 3, 1):
                block[far + near] = swap(block[far], near)
        stay = [0, 2] + fars
        order = [0, 3, 1, 2] + [far + near for far in fars for near in (0, 2, 1, 3)]
        blocks = [block[b] for b in order]
        gate_part = project(blocks, gate_held)
        up_part = project(blocks, up_held)
        outs = down(
            gate_part, across_cores(gate_part), up_part, across_cores(up_part),
            down_weight, rows, [F32 if b in stay else BF16 for b in order],
        )
        part = dict(zip(order, outs))
        sums, direct = [], []
        for far in fars:
            sums.append(add(part[far], [swap(part[far + near], near) for near in (1, 2)], BF16))
            direct.append(swap(part[far + 3], far + 3))
        pair = add(part[2], [swap(part[3], 1)], BF16, after=sums)
        part[1], sums[0] = lax.optimization_barrier((part[1], sums[0]))
        arrived = [swap(value, far) for value, far in zip(sums, fars)]
        total = add(part[0], direct, F32, 1500000000, after=[pair])
        return add(total, arrived + [swap(pair, 2), swap(part[1], 1)], BF16)

    return local


def solution(mesh):
    return jax.shard_map(
        make_local(mesh.shape["wide"], mesh.shape["narrow"]),
        mesh=mesh,
        in_specs=(
            P(("groups", "wide"), "narrow"),
            P("narrow", "wide"),
            P("narrow", "wide"),
            P("wide", "narrow"),
        ),
        out_specs=P(("groups", "wide"), "narrow"),
        check_vma=False,
    )
```

```python
import functools

import jax
import jax.numpy as jnp
from jax import lax
from jax.experimental import pallas as pl
from jax.experimental.pallas import tpu as pltpu
from jax.sharding import PartitionSpec as P

F32 = jnp.float32
BF16 = jnp.bfloat16


def call(kernel, name, out_shape, flops, vmem, *operands):
    return pl.pallas_call(
        kernel,
        out_shape=out_shape,
        compiler_params=pltpu.CompilerParams(vmem_limit_bytes=vmem),
        cost_estimate=pl.CostEstimate(flops=flops, bytes_accessed=0, transcendentals=0),
        name=name,
    )(*operands)


def fetch_kernel(pieces, source, target, sems):
    step = source.shape[0] // pieces
    copies = []
    for i in range(pieces):
        part = pl.ds(i * step, step)
        copies.append(pltpu.make_async_copy(source.at[part], target.at[part], sems.at[i]))
    for copy in copies:
        copy.start()
    for copy in copies:
        copy.wait()


def fetch(weight, grant, hint, pieces=8):
    return pl.pallas_call(
        functools.partial(fetch_kernel, pieces),
        in_specs=[pl.BlockSpec(memory_space=pl.ANY)],
        out_specs=pl.BlockSpec(memory_space=pltpu.VMEM),
        out_shape=jax.ShapeDtypeStruct(weight.shape, weight.dtype),
        scratch_shapes=[pltpu.SemaphoreType.DMA((pieces,))],
        compiler_params=pltpu.CompilerParams(vmem_limit_bytes=grant << 20),
        cost_estimate=pl.CostEstimate(flops=hint, bytes_accessed=0, transcendentals=0),
        name="fetch",
    )(weight)


def project_kernel(*refs):
    *block_refs, weight_ref, out_ref = refs
    rows = jnp.concatenate([ref[...] for ref in block_refs], axis=0)
    out_ref[...] = jnp.dot(rows, weight_ref[...], preferred_element_type=F32)


def project(blocks, weight):
    rows = sum(block.shape[0] for block in blocks)
    out = jax.ShapeDtypeStruct((rows, weight.shape[1]), F32)
    return call(project_kernel, "project", out, 400000000, 4 << 20, *blocks, weight)


def down_kernel(gate_ref, gate_other_ref, up_ref, up_other_ref, weight_ref, *out_refs):
    gate_sum = gate_ref[...] + gate_other_ref[...]
    up_sum = up_ref[...] + up_other_ref[...]
    hidden = (jax.nn.silu(gate_sum) * up_sum).astype(BF16)
    width = weight_ref.shape[1]
    tile = min(512, width)
    rows = out_refs[0].shape[0]

    def column_tile(step, carry):
        columns = pl.ds(pl.multiple_of(step * tile, tile), tile)
        partial = jnp.dot(hidden, weight_ref[:, columns], preferred_element_type=F32)
        for k, out_ref in enumerate(out_refs):
            out_ref[:, columns] = partial[k * rows:(k + 1) * rows].astype(out_ref.dtype)
        return carry

    lax.fori_loop(0, width // tile, column_tile, 0, unroll=True)


def down(gate, gate_other, up, up_other, weight, rows, dtypes):
    width = weight.shape[1]
    outs = [jax.ShapeDtypeStruct((rows, width), dtype) for dtype in dtypes]
    flops = 2 * gate.shape[0] * weight.shape[0] * width
    return call(
        down_kernel, "down", outs, flops, 4 << 20, gate, gate_other, up, up_other, weight
    )


def add_kernel(count, own_ref, *refs):
    total = own_ref[...]
    for ref in refs[:count]:
        total = total + ref[...].astype(F32)
    refs[-1][...] = total.astype(refs[-1].dtype)


def add(own, arrived, dtype, hint=1000000, after=()):
    count = len(arrived)
    return pl.pallas_call(
        functools.partial(add_kernel, count),
        in_specs=[pl.BlockSpec(memory_space=pltpu.VMEM)] * (1 + count)
        + [pl.BlockSpec(memory_space=pl.ANY)] * len(after),
        out_shape=jax.ShapeDtypeStruct(own.shape, dtype),
        compiler_params=pltpu.CompilerParams(vmem_limit_bytes=2 << 20),
        cost_estimate=pl.CostEstimate(flops=hint, bytes_accessed=0, transcendentals=0),
        name="add",
    )(own, *arrived, *after)


def make_local(wide, narrow):
    fars = list(range(4, wide, 4))

    def swap(value, bits):
        return lax.ppermute(value, "wide", [(i, i ^ bits) for i in range(wide)])

    def across_cores(value):
        return lax.ppermute(value, "narrow", [(i, (i + 1) % narrow) for i in range(narrow)])

    def local(tokens, gate_weight, up_weight, down_weight):
        rows = tokens.shape[0]
        block = {0: tokens}
        for far in fars:
            block[far] = swap(tokens, far)
        for near in (1, 2):
            block[near] = swap(tokens, near)
        gate_held = fetch(gate_weight, 48, 2000000000)
        up_held = fetch(up_weight, 48, 2000000000)
        own, gate_held = lax.optimization_barrier((tokens, gate_held))
        block[3] = swap(own, 3)
        for far in fars:
            block[far + 3] = swap(own, far + 3)
        *crossed, gate_held = lax.optimization_barrier([block[far] for far in fars] + [gate_held])
        block.update(zip(fars, crossed))
        for far in fars:
            for near in (2, 1):
                block[far + near] = swap(block[far], near)
        stay = [0, 2] + fars
        order = [0, 3, 1, 2] + [far + near for far in fars for near in (0, 2, 1, 3)]
        blocks = [block[b] for b in order]
        gate_part = project(blocks, gate_held)
        up_part = project(blocks, up_held)
        outs = down(
            gate_part, across_cores(gate_part), up_part, across_cores(up_part),
            down_weight, rows, [F32 if b in stay else BF16 for b in order],
        )
        part = dict(zip(order, outs))
        sums, direct = [], []
        for far in fars:
            sums.append(add(part[far], [swap(part[far + near], near) for near in (1, 2)], BF16))
            direct.append(swap(part[far + 3], far + 3))
        pair = add(part[2], [swap(part[3], 1)], BF16, after=sums)
        part[1], sums[0] = lax.optimization_barrier((part[1], sums[0]))
        arrived = [swap(value, far) for value, far in zip(sums, fars)]
        total = add(part[0], direct, F32, 1500000000, after=[pair])
        return add(total, arrived + [swap(pair, 2), swap(part[1], 1)], BF16)

    return local


def solution(mesh):
    return jax.shard_map(
        make_local(mesh.shape["wide"], mesh.shape["narrow"]),
        mesh=mesh,
        in_specs=(
            P(("groups", "wide"), "narrow"),
            P("narrow", "wide"),
            P("narrow", "wide"),
            P("wide", "narrow"),
        ),
        out_specs=P(("groups", "wide"), "narrow"),
        check_vma=False,
    )
```

```python
import functools

import jax
import jax.numpy as jnp
from jax import lax
from jax.experimental import pallas as pl
from jax.experimental.pallas import tpu as pltpu
from jax.sharding import PartitionSpec as P

F32 = jnp.float32
BF16 = jnp.bfloat16


def call(kernel, name, out_shape, flops, vmem, *operands):
    return pl.pallas_call(
        kernel,
        out_shape=out_shape,
        compiler_params=pltpu.CompilerParams(vmem_limit_bytes=vmem),
        cost_estimate=pl.CostEstimate(flops=flops, bytes_accessed=0, transcendentals=0),
        name=name,
    )(*operands)


def fetch_kernel(pieces, source, target, sems):
    step = source.shape[0] // pieces
    copies = []
    for i in range(pieces):
        part = pl.ds(i * step, step)
        copies.append(pltpu.make_async_copy(source.at[part], target.at[part], sems.at[i]))
    for copy in copies:
        copy.start()
    for copy in copies:
        copy.wait()


def fetch(weight, grant, hint, pieces=8):
    return pl.pallas_call(
        functools.partial(fetch_kernel, pieces),
        in_specs=[pl.BlockSpec(memory_space=pl.ANY)],
        out_specs=pl.BlockSpec(memory_space=pltpu.VMEM),
        out_shape=jax.ShapeDtypeStruct(weight.shape, weight.dtype),
        scratch_shapes=[pltpu.SemaphoreType.DMA((pieces,))],
        compiler_params=pltpu.CompilerParams(vmem_limit_bytes=grant << 20),
        cost_estimate=pl.CostEstimate(flops=hint, bytes_accessed=0, transcendentals=0),
        name="fetch",
    )(weight)


def project_kernel(*refs):
    *block_refs, weight_ref, out_ref = refs
    rows = jnp.concatenate([ref[...] for ref in block_refs], axis=0)
    out_ref[...] = jnp.dot(rows, weight_ref[...], preferred_element_type=F32)


def project(blocks, weight):
    rows = sum(block.shape[0] for block in blocks)
    out = jax.ShapeDtypeStruct((rows, weight.shape[1]), F32)
    return call(project_kernel, "project", out, 400000000, 4 << 20, *blocks, weight)


def down_kernel(gate_ref, gate_other_ref, up_ref, up_other_ref, weight_ref, *out_refs):
    gate_sum = gate_ref[...] + gate_other_ref[...]
    up_sum = up_ref[...] + up_other_ref[...]
    hidden = (jax.nn.silu(gate_sum) * up_sum).astype(BF16)
    width = weight_ref.shape[1]
    tile = min(512, width)
    rows = out_refs[0].shape[0]

    def column_tile(step, carry):
        columns = pl.ds(pl.multiple_of(step * tile, tile), tile)
        partial = jnp.dot(hidden, weight_ref[:, columns], preferred_element_type=F32)
        for k, out_ref in enumerate(out_refs):
            out_ref[:, columns] = partial[k * rows:(k + 1) * rows].astype(out_ref.dtype)
        return carry

    lax.fori_loop(0, width // tile, column_tile, 0, unroll=True)


def down(gate, gate_other, up, up_other, weight, rows, dtypes):
    width = weight.shape[1]
    outs = [jax.ShapeDtypeStruct((rows, width), dtype) for dtype in dtypes]
    flops = 2 * gate.shape[0] * weight.shape[0] * width
    return call(
        down_kernel, "down", outs, flops, 4 << 20, gate, gate_other, up, up_other, weight
    )


def add_kernel(count, own_ref, *refs):
    total = own_ref[...]
    for ref in refs[:count]:
        total = total + ref[...].astype(F32)
    refs[-1][...] = total.astype(refs[-1].dtype)


def add(own, arrived, dtype, hint=1000000, after=()):
    count = len(arrived)
    return pl.pallas_call(
        functools.partial(add_kernel, count),
        in_specs=[pl.BlockSpec(memory_space=pltpu.VMEM)] * (1 + count)
        + [pl.BlockSpec(memory_space=pl.ANY)] * len(after),
        out_shape=jax.ShapeDtypeStruct(own.shape, dtype),
        compiler_params=pltpu.CompilerParams(vmem_limit_bytes=2 << 20),
        cost_estimate=pl.CostEstimate(flops=hint, bytes_accessed=0, transcendentals=0),
        name="add",
    )(own, *arrived, *after)


def make_local(wide, narrow):
    fars = list(range(4, wide, 4))

    def swap(value, bits):
        return lax.ppermute(value, "wide", [(i, i ^ bits) for i in range(wide)])

    def across_cores(value):
        return lax.ppermute(value, "narrow", [(i, (i + 1) % narrow) for i in range(narrow)])

    def local(tokens, gate_weight, up_weight, down_weight):
        rows = tokens.shape[0]
        block = {0: tokens}
        for far in fars:
            block[far] = swap(tokens, far)
        for near in (1, 2):
            block[near] = swap(tokens, near)
        gate_held = fetch(gate_weight, 48, 2000000000)
        up_held = fetch(up_weight, 48, 2000000000)
        own, gate_held = lax.optimization_barrier((tokens, gate_held))
        block[3] = swap(block[2], 1)
        for far in fars:
            block[far + 3] = swap(own, far + 3)
        *crossed, gate_held = lax.optimization_barrier([block[far] for far in fars] + [gate_held])
        block.update(zip(fars, crossed))
        for far in fars:
            for near in (2, 1):
                block[far + near] = swap(block[far], near)
        stay = [0, 2] + fars
        order = [0, 3, 1, 2] + [far + near for far in fars for near in (0, 2, 1, 3)]
        blocks = [block[b] for b in order]
        gate_part = project(blocks, gate_held)
        up_part = project(blocks, up_held)
        outs = down(
            gate_part, across_cores(gate_part), up_part, across_cores(up_part),
            down_weight, rows, [F32 if b in stay else BF16 for b in order],
        )
        part = dict(zip(order, outs))
        sums, direct = [], []
        for far in fars:
            sums.append(add(part[far], [swap(part[far + near], near) for near in (1, 2)], BF16))
            direct.append(swap(part[far + 3], far + 3))
        pair = add(part[2], [swap(part[3], 1)], BF16, after=sums)
        part[1], sums[0] = lax.optimization_barrier((part[1], sums[0]))
        arrived = [swap(value, far) for value, far in zip(sums, fars)]
        total = add(part[0], direct, F32, 1500000000, after=[pair])
        return add(total, arrived + [swap(pair, 2), swap(part[1], 1)], BF16)

    return local


def solution(mesh):
    return jax.shard_map(
        make_local(mesh.shape["wide"], mesh.shape["narrow"]),
        mesh=mesh,
        in_specs=(
            P(("groups", "wide"), "narrow"),
            P("narrow", "wide"),
            P("narrow", "wide"),
            P("wide", "narrow"),
        ),
        out_specs=P(("groups", "wide"), "narrow"),
        check_vma=False,
    )
```

```python
import functools

import jax
import jax.numpy as jnp
from jax import lax
from jax.experimental import pallas as pl
from jax.experimental.pallas import tpu as pltpu
from jax.sharding import PartitionSpec as P

F32 = jnp.float32
BF16 = jnp.bfloat16


def call(kernel, name, out_shape, flops, vmem, *operands):
    return pl.pallas_call(
        kernel,
        out_shape=out_shape,
        compiler_params=pltpu.CompilerParams(vmem_limit_bytes=vmem),
        cost_estimate=pl.CostEstimate(flops=flops, bytes_accessed=0, transcendentals=0),
        name=name,
    )(*operands)


def fetch_kernel(pieces, source, target, sems):
    step = source.shape[0] // pieces
    copies = []
    for i in range(pieces):
        part = pl.ds(i * step, step)
        copies.append(pltpu.make_async_copy(source.at[part], target.at[part], sems.at[i]))
    for copy in copies:
        copy.start()
    for copy in copies:
        copy.wait()


def fetch(weight, grant, hint, pieces=8):
    return pl.pallas_call(
        functools.partial(fetch_kernel, pieces),
        in_specs=[pl.BlockSpec(memory_space=pl.ANY)],
        out_specs=pl.BlockSpec(memory_space=pltpu.VMEM),
        out_shape=jax.ShapeDtypeStruct(weight.shape, weight.dtype),
        scratch_shapes=[pltpu.SemaphoreType.DMA((pieces,))],
        compiler_params=pltpu.CompilerParams(vmem_limit_bytes=grant << 20),
        cost_estimate=pl.CostEstimate(flops=hint, bytes_accessed=0, transcendentals=0),
        name="fetch",
    )(weight)


def project_kernel(*refs):
    *block_refs, weight_ref, out_ref = refs
    rows = jnp.concatenate([ref[...] for ref in block_refs], axis=0)
    out_ref[...] = jnp.dot(rows, weight_ref[...], preferred_element_type=F32)


def project(blocks, weight):
    rows = sum(block.shape[0] for block in blocks)
    out = jax.ShapeDtypeStruct((rows, weight.shape[1]), F32)
    return call(project_kernel, "project", out, 400000000, 4 << 20, *blocks, weight)


def down_kernel(gate_ref, gate_other_ref, up_ref, up_other_ref, weight_ref, *out_refs):
    gate_sum = gate_ref[...] + gate_other_ref[...]
    up_sum = up_ref[...] + up_other_ref[...]
    hidden = (jax.nn.silu(gate_sum) * up_sum).astype(BF16)
    width = weight_ref.shape[1]
    tile = min(512, width)
    rows = out_refs[0].shape[0]

    def column_tile(step, carry):
        columns = pl.ds(pl.multiple_of(step * tile, tile), tile)
        partial = jnp.dot(hidden, weight_ref[:, columns], preferred_element_type=F32)
        for k, out_ref in enumerate(out_refs):
            out_ref[:, columns] = partial[k * rows:(k + 1) * rows].astype(out_ref.dtype)
        return carry

    lax.fori_loop(0, width // tile, column_tile, 0, unroll=True)


def down(gate, gate_other, up, up_other, weight, rows, dtypes):
    width = weight.shape[1]
    outs = [jax.ShapeDtypeStruct((rows, width), dtype) for dtype in dtypes]
    flops = 2 * gate.shape[0] * weight.shape[0] * width
    return call(
        down_kernel, "down", outs, flops, 4 << 20, gate, gate_other, up, up_other, weight
    )


def add_kernel(count, own_ref, *refs):
    total = own_ref[...]
    for ref in refs[:count]:
        total = total + ref[...].astype(F32)
    refs[-1][...] = total.astype(refs[-1].dtype)


def add(own, arrived, dtype, hint=1000000, after=()):
    count = len(arrived)
    return pl.pallas_call(
        functools.partial(add_kernel, count),
        in_specs=[pl.BlockSpec(memory_space=pltpu.VMEM)] * (1 + count)
        + [pl.BlockSpec(memory_space=pl.ANY)] * len(after),
        out_shape=jax.ShapeDtypeStruct(own.shape, dtype),
        compiler_params=pltpu.CompilerParams(vmem_limit_bytes=2 << 20),
        cost_estimate=pl.CostEstimate(flops=hint, bytes_accessed=0, transcendentals=0),
        name="add",
    )(own, *arrived, *after)


def make_local(wide, narrow):
    fars = list(range(4, wide, 4))

    def swap(value, bits):
        return lax.ppermute(value, "wide", [(i, i ^ bits) for i in range(wide)])

    def across_cores(value):
        return lax.ppermute(value, "narrow", [(i, (i + 1) % narrow) for i in range(narrow)])

    def local(tokens, gate_weight, up_weight, down_weight):
        rows = tokens.shape[0]
        block = {0: tokens}
        for far in fars:
            block[far] = swap(tokens, far)
        for near in (1, 2):
            block[near] = swap(tokens, near)
        gate_held = fetch(gate_weight, 48, 2000000000)
        up_held = fetch(up_weight, 48, 2000000000)
        own, gate_held = lax.optimization_barrier((tokens, gate_held))
        block[3] = swap(own, 3)
        *crossed, gate_held = lax.optimization_barrier([block[far] for far in fars] + [gate_held])
        block.update(zip(fars, crossed))
        for far in fars:
            for near in (2, 3, 1):
                block[far + near] = swap(block[far], near)
        stay = [0, 2] + fars
        order = [0, 3, 1, 2] + [far + near for far in fars for near in (0, 2, 1, 3)]
        blocks = [block[b] for b in order]
        gate_part = project(blocks, gate_held)
        up_part = project(blocks, up_held)
        outs = down(
            gate_part, across_cores(gate_part), up_part, across_cores(up_part),
            down_weight, rows, [F32 if b in stay else BF16 for b in order],
        )
        part = dict(zip(order, outs))
        sums, direct = [], []
        for far in fars:
            sums.append(add(part[far], [swap(part[far + near], near) for near in (1, 2)], BF16))
            direct.append(swap(part[far + 3], far + 3))
        pair = add(part[2], [swap(part[3], 1)], BF16)
        part[1], sums[0] = lax.optimization_barrier((part[1], sums[0]))
        arrived = [swap(value, far) for value, far in zip(sums, fars)]
        total = add(part[0], direct, F32, 1500000000, after=[pair])
        return add(total, arrived + [swap(pair, 2), swap(part[1], 1)], BF16)

    return local


def solution(mesh):
    return jax.shard_map(
        make_local(mesh.shape["wide"], mesh.shape["narrow"]),
        mesh=mesh,
        in_specs=(
            P(("groups", "wide"), "narrow"),
            P("narrow", "wide"),
            P("narrow", "wide"),
            P("wide", "narrow"),
        ),
        out_specs=P(("groups", "wide"), "narrow"),
        check_vma=False,
    )
```

```python
import functools

import jax
import jax.numpy as jnp
from jax import lax
from jax.experimental import pallas as pl
from jax.experimental.pallas import tpu as pltpu
from jax.sharding import PartitionSpec as P

F32 = jnp.float32
BF16 = jnp.bfloat16


def call(kernel, name, out_shape, flops, vmem, *operands):
    return pl.pallas_call(
        kernel,
        out_shape=out_shape,
        compiler_params=pltpu.CompilerParams(vmem_limit_bytes=vmem),
        cost_estimate=pl.CostEstimate(flops=flops, bytes_accessed=0, transcendentals=0),
        name=name,
    )(*operands)


def fetch_kernel(pieces, source, target, sems):
    step = source.shape[0] // pieces
    copies = []
    for i in range(pieces):
        part = pl.ds(i * step, step)
        copies.append(pltpu.make_async_copy(source.at[part], target.at[part], sems.at[i]))
    for copy in copies:
        copy.start()
    for copy in copies:
        copy.wait()


def fetch(weight, grant, hint, pieces=8):
    return pl.pallas_call(
        functools.partial(fetch_kernel, pieces),
        in_specs=[pl.BlockSpec(memory_space=pl.ANY)],
        out_specs=pl.BlockSpec(memory_space=pltpu.VMEM),
        out_shape=jax.ShapeDtypeStruct(weight.shape, weight.dtype),
        scratch_shapes=[pltpu.SemaphoreType.DMA((pieces,))],
        compiler_params=pltpu.CompilerParams(vmem_limit_bytes=grant << 20),
        cost_estimate=pl.CostEstimate(flops=hint, bytes_accessed=0, transcendentals=0),
        name="fetch",
    )(weight)


def project_kernel(*refs):
    *block_refs, weight_ref, out_ref = refs
    rows = jnp.concatenate([ref[...] for ref in block_refs], axis=0)
    out_ref[...] = jnp.dot(rows, weight_ref[...], preferred_element_type=F32)


def project(blocks, weight):
    rows = sum(block.shape[0] for block in blocks)
    out = jax.ShapeDtypeStruct((rows, weight.shape[1]), F32)
    return call(project_kernel, "project", out, 400000000, 4 << 20, *blocks, weight)


def down_kernel(gate_ref, gate_other_ref, up_ref, up_other_ref, weight_ref, *out_refs):
    gate_sum = gate_ref[...] + gate_other_ref[...]
    up_sum = up_ref[...] + up_other_ref[...]
    hidden = (jax.nn.silu(gate_sum) * up_sum).astype(BF16)
    width = weight_ref.shape[1]
    tile = min(512, width)
    rows = out_refs[0].shape[0]

    def column_tile(step, carry):
        columns = pl.ds(pl.multiple_of(step * tile, tile), tile)
        partial = jnp.dot(hidden, weight_ref[:, columns], preferred_element_type=F32)
        for k, out_ref in enumerate(out_refs):
            out_ref[:, columns] = partial[k * rows:(k + 1) * rows].astype(out_ref.dtype)
        return carry

    lax.fori_loop(0, width // tile, column_tile, 0, unroll=True)


def down(gate, gate_other, up, up_other, weight, rows, dtypes):
    width = weight.shape[1]
    outs = [jax.ShapeDtypeStruct((rows, width), dtype) for dtype in dtypes]
    flops = 2 * gate.shape[0] * weight.shape[0] * width
    return call(
        down_kernel, "down", outs, flops, 4 << 20, gate, gate_other, up, up_other, weight
    )


def add_kernel(count, own_ref, *refs):
    total = own_ref[...]
    for ref in refs[:count]:
        total = total + ref[...].astype(F32)
    refs[-1][...] = total.astype(refs[-1].dtype)


def add(own, arrived, dtype, hint=1000000, after=()):
    count = len(arrived)
    return pl.pallas_call(
        functools.partial(add_kernel, count),
        in_specs=[pl.BlockSpec(memory_space=pltpu.VMEM)] * (1 + count)
        + [pl.BlockSpec(memory_space=pl.ANY)] * len(after),
        out_shape=jax.ShapeDtypeStruct(own.shape, dtype),
        compiler_params=pltpu.CompilerParams(vmem_limit_bytes=2 << 20),
        cost_estimate=pl.CostEstimate(flops=hint, bytes_accessed=0, transcendentals=0),
        name="add",
    )(own, *arrived, *after)


def make_local(wide, narrow):
    fars = list(range(4, wide, 4))

    def swap(value, bits):
        return lax.ppermute(value, "wide", [(i, i ^ bits) for i in range(wide)])

    def across_cores(value):
        return lax.ppermute(value, "narrow", [(i, (i + 1) % narrow) for i in range(narrow)])

    def local(tokens, gate_weight, up_weight, down_weight):
        rows = tokens.shape[0]
        block = {0: tokens}
        for far in fars:
            block[far] = swap(tokens, far)
        for near in (1, 2):
            block[near] = swap(tokens, near)
        gate_held = fetch(gate_weight, 48, 2000000000)
        up_held = fetch(up_weight, 48, 2000000000)
        own, gate_held = lax.optimization_barrier((tokens, gate_held))
        block[3] = swap(own, 3)
        *crossed, gate_held = lax.optimization_barrier([block[far] for far in fars] + [gate_held])
        block.update(zip(fars, crossed))
        for far in fars:
            for near in (2, 3, 1):
                block[far + near] = swap(block[far], near)
        stay = [0, 2] + fars
        order = [0, 3, 1, 2] + [far + near for far in fars for near in (0, 2, 1, 3)]
        blocks = [block[b] for b in order]
        gate_part = project(blocks, gate_held)
        up_part = project(blocks, up_held)
        outs = down(
            gate_part, across_cores(gate_part), up_part, across_cores(up_part),
            down_weight, rows, [F32 if b in stay else BF16 for b in order],
        )
        part = dict(zip(order, outs))
        sums, direct = [], []
        for far in fars:
            sums.append(add(part[far], [swap(part[far + near], near) for near in (2, 1)], BF16))
            direct.append(swap(part[far + 3], far + 3))
        pair = add(part[2], [swap(part[3], 1)], BF16, after=sums)
        part[1], sums[0] = lax.optimization_barrier((part[1], sums[0]))
        arrived = [swap(value, far) for value, far in zip(sums, fars)]
        total = add(part[0], direct, F32, 1500000000, after=[pair])
        return add(total, arrived + [swap(pair, 2), swap(part[1], 1)], BF16)

    return local


def solution(mesh):
    return jax.shard_map(
        make_local(mesh.shape["wide"], mesh.shape["narrow"]),
        mesh=mesh,
        in_specs=(
            P(("groups", "wide"), "narrow"),
            P("narrow", "wide"),
            P("narrow", "wide"),
            P("wide", "narrow"),
        ),
        out_specs=P(("groups", "wide"), "narrow"),
        check_vma=False,
    )
```
